256 devices in a mesh: gx: 64 (over y, z, core), gy: 4 (over x).
Axes of the slice: x: 4, y: 4, z: 8, core: 2. Of those that a mesh axis runs over, the one named last changes fastest.
Arguments:
- cotangent: float32 [512, 512, 128], P('gx', 'gy'), may hold values from -8 to 8
- capacity: float32 [512, 512, 128], P('gx', 'gy'), may hold values from 0.2 to 2
- conductivity: float32 [512, 512, 128], P('gx', 'gy'), may hold values from 0.5 to 2
- surface_gap: float32 [512, 512], P('gx', 'gy'), may hold values from 0.5 to 2
- transfer_coeff: float32 [2048], replicated, may hold values from 0.25 to 2
- segment_ids: int32 [512, 64], P('gx', 'gy'), may hold values from 0 to 2047
Outputs:
- adjoint: float32 [512, 512, 128], P('gx', 'gy')
- coeff_gradient: float32 [2048], P(('gx', 'gy'))
The draws below stay inside these ranges and needn't reach their ends.
All inputs are finite; a program needn't handle non-finite values.
Results may differ from the reference program's by a relative error of at most 0.00002.
Values sent between devices are 32-bit elements; how exact they have to be, the bound alone decides.
A program may use at most 128 MiB of HBM per device.

```python
import math
import jax
import jax.numpy as jnp
import numpy as np

CZ = 128
FB = 8
ITERS = 8
NX = 512
NY = 512
NSEG = 2048


def with_ends(array, stream_key, smallest, largest):
    longest = array.shape.index(max(array.shape))
    spots = []
    for shift in (0, 1):
        where = [jax.random.randint(jax.random.fold_in(stream_key, axis), (), 0, length) for axis, length in enumerate(array.shape)]
        where[longest] = (where[longest] + shift) % array.shape[longest]
        spots.append(tuple(where))
    return array.at[spots[0]].set(smallest).at[spots[1]].set(largest)


def block_levels(key, shape, cuts, smallest, top_value):
    gain, own = 1.0, jax.random.fold_in(key, 6)
    for position, parts in cuts:
        draws = jnp.exp(jax.random.uniform(jax.random.fold_in(own, position), (parts,), jnp.float32, smallest / len(cuts), top_value / len(cuts)))
        gain = gain * jnp.repeat(draws, shape[position] // parts).reshape([-1 if axis == position else 1 for axis in range(len(shape))])
    return gain


def rank_table(number_of, lean):
    weights = [(1 << 20) // math.isqrt(grade ** lean) + 1 for grade in range(1, number_of + 1)]
    scale = 1 + sum(weights) // (1 << 30)
    return np.cumsum(np.array([max(1, weight // scale) for weight in weights]))


def skewed_ids(own_key, extent, number_of, slope):
    grid = rank_table(number_of, slope)
    lot = jax.random.randint(jax.random.fold_in(own_key, 1), extent, 0, int(grid[number_of - 1]))
    rank = jnp.searchsorted(jnp.asarray(grid, jnp.int32), lot, side="right")
    return jax.random.permutation(jax.random.fold_in(own_key, 2), number_of)[rank].astype(jnp.int32)


def gaussian(rng, extent, spread, limit, cuts=(), held_as=jnp.bfloat16):
    loudness = block_levels(rng, extent, cuts, -0.22, 0.18) if cuts else 1.0
    result = jax.random.normal(rng, extent, jnp.float32) * spread * loudness
    return jnp.minimum(jnp.maximum(result, -limit), limit).astype(held_as)


def setup_inputs(seed: int = 0) -> dict:
    splits = jax.random.split(jax.random.key(seed), 7)
    cotangent = gaussian(splits[0], (NX, NY, CZ), 1.0, 8.0, ((0, 64), (1, 4)), jnp.float32)
    capacity = jnp.clip(jnp.exp(math.log(2.0) - 2.3025851 * jax.random.uniform(splits[1], (NX, NY, CZ), jnp.float32) ** block_levels(splits[1], (NX, NY, CZ), ((0, 64), (1, 4)), -0.2, 0.2)), 0.2, 2.0)
    conductivity = jnp.clip(0.5 + 1.5 * jax.random.uniform(splits[2], (NX, NY, CZ), jnp.float32) ** block_levels(splits[2], (NX, NY, CZ), ((0, 64), (1, 4)), -0.2, 0.2), 0.5, 2.0)
    surface_gap = jnp.clip(0.5 + 1.5 * jax.random.uniform(splits[3], (NX, NY), jnp.float32) ** block_levels(splits[3], (NX, NY), ((0, 64), (1, 4)), -0.2, 0.2), 0.5, 2.0)
    transfer_coeff = jnp.clip(jax.random.uniform(splits[4], (NSEG,), jnp.float32, 0.25, 2.0), 0.25, 2.0)
    segment_ids = with_ends(skewed_ids(splits[5], (NX, NY // FB), NSEG, 1), jax.random.fold_in(splits[5], 3), 0, NSEG - 1).astype(jnp.int32)
    return {"cotangent": cotangent, "capacity": capacity, "conductivity": conductivity, "surface_gap": surface_gap, "transfer_coeff": transfer_coeff, "segment_ids": segment_ids}


LOW_BOUND = 0.2
HIGH_BOUND = 28.0
CENTRE_VALUE = (HIGH_BOUND + LOW_BOUND) / 2.0
HALF_SPREAD = (HIGH_BOUND - LOW_BOUND) / 2.0
SIGMA_RATIO = CENTRE_VALUE / HALF_SPREAD


def apply_operator(field, diagonal, cond):
    centre = field[1:-1, 1:-1]
    centre_cond = cond[1:-1, 1:-1]
    accumulated = diagonal[1:-1, 1:-1] * centre
    others = ((field[2:, 1:-1], cond[2:, 1:-1]), (field[:-2, 1:-1], cond[:-2, 1:-1]),
              (field[1:-1, 2:], cond[1:-1, 2:]), (field[1:-1, :-2], cond[1:-1, :-2]))
    for other_field, other_cond in others:
        accumulated = accumulated + 0.5 * (centre_cond + other_cond) * (centre - other_field)
    vertical_field = jnp.pad(centre, ((0, 0), (0, 0), (1, 1)))
    vertical_cond = jnp.pad(centre_cond, ((0, 0), (0, 0), (1, 1)))
    for window in (slice(2, None), slice(0, -2)):
        accumulated = accumulated + 0.5 * (centre_cond + vertical_cond[:, :, window]) * (centre - vertical_field[:, :, window])
    return accumulated


def pad_sides(field):
    return jnp.pad(field, ((1, 1), (1, 1), (0, 0)))


def reference(cotangent, capacity, conductivity, surface_gap, transfer_coeff, segment_ids):
    face_coeff = jnp.repeat(jnp.take(transfer_coeff, segment_ids, axis=0), FB, axis=1)
    diagonal = capacity + jnp.pad(face_coeff[:, :, None], ((0, 0), (0, 0), (0, CZ - 1)))
    diag_padded = pad_sides(diagonal)
    cond_padded = pad_sides(conductivity)
    adjoint = jnp.zeros_like(cotangent)
    residual = cotangent
    direction = residual / CENTRE_VALUE
    ratio_prev = 1.0 / SIGMA_RATIO
    for iteration in range(ITERS):
        adjoint = adjoint + direction
        residual = residual - apply_operator(pad_sides(direction), diag_padded, cond_padded)
        if iteration + 1 < ITERS:
            ratio_new = 1.0 / (2.0 * SIGMA_RATIO - ratio_prev)
            direction = (ratio_new * ratio_prev) * direction + (2.0 * ratio_new / HALF_SPREAD) * residual
            ratio_prev = ratio_new
    face_terms = adjoint[:, :, 0] * surface_gap
    block_sums = face_terms.reshape(face_terms.shape[0], face_terms.shape[1] // FB, FB).sum(axis=2)
    summed = jax.ops.segment_sum(block_sums.reshape(-1), segment_ids.reshape(-1), num_segments=NSEG)
    return adjoint, -summed
```

```python
import functools

import jax
import jax.numpy as jnp
from jax import lax
from jax.experimental import pallas as pl
from jax.experimental.pallas import tpu as pltpu
from jax.sharding import PartitionSpec as P

MESH = pl.DeviceIdType.MESH
F32 = jnp.float32
ITERS = 8
LOW_BOUND = 0.2
HIGH_BOUND = 28.0
THETA = (HIGH_BOUND + LOW_BOUND) / 2.0
DELTA = (HIGH_BOUND - LOW_BOUND) / 2.0
SIGMA = THETA / DELTA

ROWS, COLS, LANES = 8, 128, 128
DEPTH = 3
SIDE = 8
WIDE = COLS + 2 * SIDE
TALL = ROWS + 2 * DEPTH
OWN_ROWS = pl.ds(DEPTH, ROWS)
OWN_COLS = pl.ds(SIDE, COLS)


def coefficients():
    ratio = 1.0 / SIGMA
    out = []
    for _ in range(ITERS - 1):
        new = 1.0 / (2.0 * SIGMA - ratio)
        out.append((new * ratio, 2.0 * new / DELTA))
        ratio = new
    return out


COEF = coefficients()


def kernel(
    cot, cap, cond, gap_in, tc_in, ids_in,
    out, grad,
    B, C, G, DG, WX, WYp, WYm, WZp, WZm, X, gap, tc, ids, hot, idrow, face, part, got1, row2, got2,
    loc_sem, st_send, st_recv, x_send, x_recv, r_send, r_recv,
):
    gx, gy = lax.axis_index("gx"), lax.axis_index("gy")
    nx, ny = 64, 4
    my_y, my_z, my_c = gx // 16, lax.rem(gx // 2, 8), lax.rem(gx, 2)

    def at(dx, dy):
        return (lax.rem(gx + dx + nx, nx), lax.rem(gy + dy + ny, ny))

    def plane(h):
        return (lax.rem(my_y + h // 4, 4) * 16 + my_z * 2 + my_c, lax.rem(gy + h % 4, 4))

    def column(h):
        return (my_y * 16 + lax.rem(my_z + h // 2, 8) * 2 + lax.rem(my_c + h % 2, 2), gy)

    barrier = pltpu.get_barrier_semaphore()
    around = [(dx, dy) for dx in (-1, 0, 1) for dy in (-1, 0, 1) if dx or dy]
    partners = [at(*d) for d in around] + [plane(h) for h in range(1, 16)] + [column(h) for h in range(1, 16)]
    for dev in partners:
        pl.semaphore_signal(barrier, inc=1, device_id=dev, device_id_type=MESH)

    loads = [
        pltpu.make_async_copy(cot, B.at[OWN_ROWS, OWN_COLS], loc_sem.at[0]),
        pltpu.make_async_copy(cond, C.at[OWN_ROWS, OWN_COLS], loc_sem.at[1]),
        pltpu.make_async_copy(cap, G.at[OWN_ROWS, OWN_COLS], loc_sem.at[2]),
        pltpu.make_async_copy(gap_in, gap, loc_sem.at[3]),
        pltpu.make_async_copy(tc_in, tc, loc_sem.at[4]),
        pltpu.make_async_copy(ids_in, ids, loc_sem.at[5]),
    ]
    for cp in loads:
        cp.start()

    pl.semaphore_wait(barrier, len(partners))

    sends = []
    counter = [0]

    def push(src, dst, dev):
        k = counter[0]
        counter[0] += 1
        cp = pltpu.make_async_remote_copy(
            src, dst, st_send.at[k], st_recv.at[k], device_id=dev, device_id_type=MESH
        )
        cp.start()
        sends.append(cp)
        return cp

    def rows_for(dx, depth_from, count):
        if dx > 0:
            first = ROWS - (depth_from + count - 1)
            return pl.ds(first, count), pl.ds(DEPTH - (depth_from + count - 1), count)
        return pl.ds(depth_from - 1, count), pl.ds(DEPTH + ROWS + depth_from - 1, count)

    def cols_for(dy):
        if dy > 0:
            return pl.ds(COLS - SIDE, SIDE), pl.ds(0, SIDE)
        if dy < 0:
            return pl.ds(0, SIDE), pl.ds(SIDE + COLS, SIDE)
        return pl.ds(0, COLS), OWN_COLS

    near, first, second = [], [], []
    pairs = ((cot, B), (cond, C))
    for src, dst in pairs:
        for dy in (1, -1):
            sc, dc = cols_for(dy)
            near.append(push(src.at[:, sc], dst.at[OWN_ROWS, dc], at(0, dy)))
    for src, dst in pairs:
        for dx in (1, -1):
            sr, dr = rows_for(dx, 1, 2)
            first.append(push(src.at[sr], dst.at[dr, OWN_COLS], at(dx, 0)))
    for src, dst in pairs:
        for dx in (1, -1):
            for dy in (1, -1):
                sr, dr = rows_for(dx, 1, 3)
                sc, dc = cols_for(dy)
                first.append(push(src.at[sr, sc], dst.at[dr, dc], at(dx, dy)))

    for k in (2, 4, 5):
        loads[k].wait()
    lane8 = lax.broadcasted_iota(jnp.int32, (8, LANES), 1)
    lane1 = lax.broadcasted_iota(jnp.int32, (1, LANES), 1)

    def face_row(i, _):
        vec = jnp.zeros((1, LANES), jnp.int32)
        for jb in range(16):
            seg = ids[i, jb]
            value = tc[seg]
            cols = pl.ds(SIDE + 8 * jb, 8)
            G[DEPTH + i, cols, :] = G[DEPTH + i, cols, :] + jnp.where(lane8 == 0, value, 0.0)
            vec = jnp.where(lane1 // 8 == jb, seg, vec)
        idrow[i, :, :] = vec
        return 0

    lax.fori_loop(0, ROWS, face_row, 0)

    for dy in (1, -1):
        sc, dc = cols_for(dy)
        src_cols = pl.ds(SIDE + sc.start, sc.size)
        near.append(push(G.at[OWN_ROWS, src_cols], G.at[OWN_ROWS, dc], at(0, dy)))
    for dx in (1, -1):
        sr, dr = rows_for(dx, 1, 1)
        first.append(push(G.at[pl.ds(DEPTH + sr.start, 1), OWN_COLS], G.at[dr, OWN_COLS], at(dx, 0)))
    for dx in (1, -1):
        for dy in (1, -1):
            sr, dr = rows_for(dx, 1, 2)
            sc, dc = cols_for(dy)
            first.append(
                push(
                    G.at[pl.ds(DEPTH + sr.start, 2), pl.ds(SIDE + sc.start, SIDE)],
                    G.at[dr, dc],
                    at(dx, dy),
                )
            )
    for src, dst in pairs:
        for dx in (1, -1):
            sr, dr = rows_for(dx, 3, 1)
            second.append(push(src.at[sr], dst.at[dr, OWN_COLS], at(dx, 0)))
    for dx in (1, -1):
        sr, dr = rows_for(dx, 2, 1)
        second.append(push(G.at[pl.ds(DEPTH + sr.start, 1), OWN_COLS], G.at[dr, OWN_COLS], at(dx, 0)))

    col = lax.broadcasted_iota(jnp.int32, (WIDE, LANES), 0)
    lane = lax.broadcasted_iota(jnp.int32, (WIDE, LANES), 1)
    left_edge = jnp.logical_and(col == SIDE, gy == 0)
    right_edge = jnp.logical_and(col == SIDE + COLS - 1, gy == ny - 1)

    def setup(r):
        centre = C[r]
        up = jnp.where(jnp.logical_and(r == DEPTH + ROWS - 1, gx == nx - 1), 0.0, C[r + 1])
        down = jnp.where(jnp.logical_and(r == DEPTH, gx == 0), 0.0, C[r - 1])
        right = jnp.where(right_edge, 0.0, pltpu.roll(centre, WIDE - 1, 0))
        left = jnp.where(left_edge, 0.0, pltpu.roll(centre, 1, 0))
        above = jnp.where(lane == LANES - 1, 0.0, pltpu.roll(centre, LANES - 1, 1))
        below = jnp.where(lane == 0, 0.0, pltpu.roll(centre, 1, 1))
        DG[r] = G[r] + (3.0 * centre + 0.5 * ((up + down) + (right + left) + (above + below)))
        WYp[r] = jnp.where(right_edge, 0.0, 0.5 * (centre + right))
        WYm[r] = jnp.where(left_edge, 0.0, 0.5 * (centre + left))
        WZp[r] = jnp.where(lane == LANES - 1, 0.0, 0.5 * (centre + above))
        WZm[r] = jnp.where(lane == 0, 0.0, 0.5 * (centre + below))
        outer = jnp.logical_or(
            jnp.logical_and(r == DEPTH + ROWS - 1, gx == nx - 1), jnp.logical_and(r == DEPTH - 1, gx == 0)
        )
        WX[r] = jnp.where(outer, 0.0, 0.5 * (centre + up))

    def setup_low(r):
        centre = C[r]
        WX[r - 1] = jnp.where(jnp.logical_and(r == DEPTH, gx == 0), 0.0, 0.5 * (centre + C[r - 1]))

    def step(n, r):
        a, beta = COEF[n - 1]
        src = B if n == 1 else X.at[n - 2]
        x = src[r]
        acc = WX[r] * src[r + 1] + WX[r - 1] * src[r - 1]
        acc += WYp[r] * pltpu.roll(x, WIDE - 1, 0) + WYm[r] * pltpu.roll(x, 1, 0)
        acc += WZp[r] * pltpu.roll(x, LANES - 1, 1) + WZm[r] * pltpu.roll(x, 1, 1)
        acc = acc - DG[r] * x
        if n == 1:
            return ((1.0 + a) / THETA + beta) * x + (beta / THETA) * acc
        b = B[r]
        if n == 2:
            return (1.0 + a) * x + (beta - a / THETA) * b + beta * acc
        return (1.0 + a) * x - a * X[n - 3, r] + beta * (b + acc)

    def run(n, rows):
        for i in rows:
            new = step(n, i + DEPTH)
            if n < ITERS - 1:
                X[n - 1, i + DEPTH] = new
            else:
                own = new[SIDE : SIDE + COLS]
                out[i] = own
                acc = jnp.zeros((8, LANES), F32)
                for jb in range(16):
                    piece = jnp.where(lane8 == 0, own[8 * jb : 8 * jb + 8], 0.0)
                    acc = acc + pltpu.roll(piece, 8 * jb, 1, stride=1, stride_axis=0)
                face[i] = jnp.sum(acc, axis=0, keepdims=True) * gap[i : i + 1, :]

    x_copies = {}

    def send_x(n):
        for side, dx, src_row, dst_row in ((0, 1, 5, 0), (1, -1, 2, TALL - 1)):
            cp = pltpu.make_async_remote_copy(
                X.at[n - 2, DEPTH + src_row], X.at[n - 2, dst_row],
                x_send.at[side, n - 2], x_recv.at[side, n - 2],
                device_id=at(dx, 0), device_id_type=MESH,
            )
            cp.start()
            x_copies[side, n] = cp

    loads[0].wait()
    loads[1].wait()
    loads[3].wait()
    for cp in near:
        cp.wait_recv()
    setup_low(1 + DEPTH)
    for i in range(1, 7):
        setup(i + DEPTH)
    run(1, range(1, 7))
    send_x(2)
    run(2, range(2, 6))
    send_x(3)
    run(3, (3, 4))

    sub128 = lax.broadcasted_iota(jnp.int32, (LANES, LANES), 0)

    def one_hot(i, _):
        seg = idrow[i]
        low = ((seg >> 5) & 15) * 8 + (seg & 7)
        hot[i] = jnp.where(sub128 == low, 1.0, 0.0).astype(jnp.bfloat16)
        return 0

    lax.fori_loop(0, ROWS, one_hot, 0)

    for cp in first:
        cp.wait_recv()
    setup_low(-1 + DEPTH)
    for i in (-1, 0, 7, 8):
        setup(i + DEPTH)
    run(1, (-1, 0, 7, 8))
    run(2, (0, 1, 6, 7))
    run(3, (1, 2, 5, 6))
    send_x(4)
    run(4, (2, 3, 4, 5))
    send_x(5)
    run(5, (3, 4))

    for cp in second:
        cp.wait_recv()
    setup_low(-2 + DEPTH)
    for i in (-2, 9):
        setup(i + DEPTH)
    run(1, (-2, 9))
    run(2, (-1, 8))
    run(3, (0, 7))
    run(4, (1, 6))
    run(5, (2, 5))
    run(6, (3, 4))

    for n in (2, 3):
        for side in (0, 1):
            x_copies[side, n].wait_recv()
    run(2, (-2, 9))
    run(3, (-2, -1, 8, 9))
    run(4, (-1, 0, 7, 8))
    run(5, (0, 1, 6, 7))
    run(6, (1, 2, 5, 6))
    run(7, (2, 3, 4, 5))

    for side in (0, 1):
        x_copies[side, 4].wait_recv()
    run(4, (-2, 9))
    run(5, (-1, 8))
    run(6, (0, 7))
    run(7, (1, 6))

    for side in (0, 1):
        x_copies[side, 5].wait_recv()
    run(5, (-2, 9))
    run(6, (-1, 8))
    run(7, (0, 7))

    sub16 = lax.broadcasted_iota(jnp.int32, (16, LANES), 0)
    total = jnp.zeros((48, LANES), F32)
    for i in range(ROWS):
        seg = idrow[i]
        high = (seg >> 9) * 4 + ((seg >> 3) & 3)
        value = jnp.where(sub16 == high, face[i], 0.0)
        v1 = value.astype(jnp.bfloat16).astype(F32)
        v2 = (value - v1).astype(jnp.bfloat16).astype(F32)
        v3 = value - v1 - v2
        left = jnp.concatenate([v1, v2, v3], axis=0).astype(jnp.bfloat16)
        total = total + lax.dot_general(
            left, hot[i], (((1,), (1,)), ((), ())), preferred_element_type=F32
        )
    sums = total[0:16] + total[16:32] + total[32:48]
    for h in range(16):
        part[h] = sums[h : h + 1, :]

    copies = []
    for h in range(1, 16):
        dev = plane(h)
        row = (dev[0] // 16) * 4 + dev[1]
        cp = pltpu.make_async_remote_copy(
            part.at[row], got1.at[h], r_send.at[0, h], r_recv.at[0, h], device_id=dev, device_id_type=MESH
        )
        cp.start()
        copies.append(cp)
    acc = part[my_y * 4 + gy]
    for h, cp in enumerate(copies, 1):
        cp.wait_recv()
        acc = acc + got1[h]
    row2[...] = acc
    more = []
    for h in range(1, 16):
        cp = pltpu.make_async_remote_copy(
            row2, got2.at[h], r_send.at[1, h], r_recv.at[1, h], device_id=column(h), device_id_type=MESH
        )
        cp.start()
        more.append(cp)
    for h, cp in enumerate(more, 1):
        cp.wait_recv()
        acc = acc + got2[h]
    place = (my_z * 2 + my_c) * 8
    spread = jnp.broadcast_to(acc, (8, LANES))
    grad[...] = -pltpu.roll(spread, lax.rem(LANES - place, LANES), 1)

    for cp in sends + list(x_copies.values()) + copies + more:
        cp.wait_send()


def body(cot, cap, cond, gap, tc, ids):
    wide = pltpu.VMEM((TALL, WIDE, LANES), F32)
    n_static = 8 + 8 + 4 + 2 + 2 + 4 + 4 + 2
    adjoint, grad = pl.pallas_call(
        kernel,
        out_shape=(
            jax.ShapeDtypeStruct((ROWS, COLS, LANES), F32),
            jax.ShapeDtypeStruct((8, LANES), F32),
        ),
        in_specs=[pl.BlockSpec(memory_space=pl.ANY)] * 6,
        out_specs=(pl.BlockSpec(memory_space=pltpu.VMEM), pl.BlockSpec(memory_space=pltpu.VMEM)),
        scratch_shapes=[wide] * 9
        + [
            pltpu.VMEM((ITERS - 2, TALL, WIDE, LANES), F32),
            pltpu.VMEM((ROWS, COLS), F32),
            pltpu.SMEM((2048,), F32),
            pltpu.SMEM((ROWS, 16), jnp.int32),
            pltpu.VMEM((ROWS, LANES, LANES), jnp.bfloat16),
            pltpu.VMEM((ROWS, 1, LANES), jnp.int32),
            pltpu.VMEM((ROWS, 1, LANES), F32),
            pltpu.VMEM((16, 1, LANES), F32),
            pltpu.VMEM((16, 1, LANES), F32),
            pltpu.VMEM((1, LANES), F32),
            pltpu.VMEM((16, 1, LANES), F32),
            pltpu.SemaphoreType.DMA((6,)),
            pltpu.SemaphoreType.DMA((n_static,)),
            pltpu.SemaphoreType.DMA((n_static,)),
            pltpu.SemaphoreType.DMA((2, 4)),
            pltpu.SemaphoreType.DMA((2, 4)),
            pltpu.SemaphoreType.DMA((2, 16)),
            pltpu.SemaphoreType.DMA((2, 16)),
        ],
        compiler_params=pltpu.CompilerParams(
            collective_id=0, has_side_effects=True, vmem_limit_bytes=48 * 1024 * 1024
        ),
    )(cot, cap, cond, gap, tc, ids)
    return adjoint, grad[0, 0:8]


def solution(mesh):
    in_specs = (
        P("gx", "gy", None),
        P("gx", "gy", None),
        P("gx", "gy", None),
        P("gx", "gy"),
        P(),
        P("gx", "gy"),
    )
    out_specs = (P("gx", "gy", None), P(("gx", "gy")))
    return jax.shard_map(body, mesh=mesh, in_specs=in_specs, out_specs=out_specs, check_vma=False)
```

```python
import functools

import jax
import jax.numpy as jnp
from jax import lax
from jax.experimental import pallas as pl
from jax.experimental.pallas import tpu as pltpu
from jax.sharding import PartitionSpec as P

MESH = pl.DeviceIdType.MESH
F32 = jnp.float32
ITERS = 8
LOW_BOUND = 0.2
HIGH_BOUND = 28.0
THETA = (HIGH_BOUND + LOW_BOUND) / 2.0
DELTA = (HIGH_BOUND - LOW_BOUND) / 2.0
SIGMA = THETA / DELTA

ROWS, COLS, LANES = 8, 128, 128
DEPTH = 3
SIDE = 8
WIDE = COLS + 2 * SIDE
TALL = ROWS + 2 * DEPTH
OWN_ROWS = pl.ds(DEPTH, ROWS)
OWN_COLS = pl.ds(SIDE, COLS)


def coefficients():
    ratio = 1.0 / SIGMA
    out = []
    for _ in range(ITERS - 1):
        new = 1.0 / (2.0 * SIGMA - ratio)
        out.append((new * ratio, 2.0 * new / DELTA))
        ratio = new
    return out


COEF = coefficients()


def kernel(
    cot, cap, cond, gap_in, tc_in, ids_in,
    out, grad,
    B, C, G, DG, WX, WYp, WYm, WZp, WZm, X, gap, tc, ids, hot, idrow, face, part, got1, row2, got2,
    loc_sem, st_send, st_recv, x_send, x_recv, r_send, r_recv,
):
    gx, gy = lax.axis_index("gx"), lax.axis_index("gy")
    nx, ny = 64, 4
    my_y, my_z, my_c = gx // 16, lax.rem(gx // 2, 8), lax.rem(gx, 2)

    def at(dx, dy):
        return (lax.rem(gx + dx + nx, nx), lax.rem(gy + dy + ny, ny))

    def plane(h):
        return (lax.rem(my_y + h // 4, 4) * 16 + my_z * 2 + my_c, lax.rem(gy + h % 4, 4))

    def column(h):
        return (my_y * 16 + lax.rem(my_z + h // 2, 8) * 2 + lax.rem(my_c + h % 2, 2), gy)

    barrier = pltpu.get_barrier_semaphore()
    around = [(dx, dy) for dx in (-1, 0, 1) for dy in (-1, 0, 1) if dx or dy]
    partners = [at(*d) for d in around] + [plane(h) for h in range(1, 16)] + [column(h) for h in range(1, 16)]
    for dev in partners:
        pl.semaphore_signal(barrier, inc=1, device_id=dev, device_id_type=MESH)

    loads = [
        pltpu.make_async_copy(cot, B.at[OWN_ROWS, OWN_COLS], loc_sem.at[0]),
        pltpu.make_async_copy(cond, C.at[OWN_ROWS, OWN_COLS], loc_sem.at[1]),
        pltpu.make_async_copy(cap, G.at[OWN_ROWS, OWN_COLS], loc_sem.at[2]),
        pltpu.make_async_copy(gap_in, gap, loc_sem.at[3]),
        pltpu.make_async_copy(tc_in, tc, loc_sem.at[4]),
        pltpu.make_async_copy(ids_in, ids, loc_sem.at[5]),
    ]
    for cp in loads:
        cp.start()

    pl.semaphore_wait(barrier, len(partners))

    sends = []
    counter = [0]

    def push(src, dst, dev):
        k = counter[0]
        counter[0] += 1
        cp = pltpu.make_async_remote_copy(
            src, dst, st_send.at[k], st_recv.at[k], device_id=dev, device_id_type=MESH
        )
        cp.start()
        sends.append(cp)
        return cp

    def rows_for(dx, depth_from, count):
        if dx > 0:
            first = ROWS - (depth_from + count - 1)
            return pl.ds(first, count), pl.ds(DEPTH - (depth_from + count - 1), count)
        return pl.ds(depth_from - 1, count), pl.ds(DEPTH + ROWS + depth_from - 1, count)

    def cols_for(dy):
        if dy > 0:
            return pl.ds(COLS - SIDE, SIDE), pl.ds(0, SIDE)
        if dy < 0:
            return pl.ds(0, SIDE), pl.ds(SIDE + COLS, SIDE)
        return pl.ds(0, COLS), OWN_COLS

    near, first, second = [], [], []
    pairs = ((cot, B), (cond, C))
    for src, dst in pairs:
        for dy in (1, -1):
            sc, dc = cols_for(dy)
            near.append(push(src.at[:, sc], dst.at[OWN_ROWS, dc], at(0, dy)))
    for src, dst in pairs:
        for dx in (1, -1):
            sr, dr = rows_for(dx, 1, 2)
            first.append(push(src.at[sr], dst.at[dr, OWN_COLS], at(dx, 0)))
    for src, dst in pairs:
        for dx in (1, -1):
            for dy in (1, -1):
                sr, dr = rows_for(dx, 1, 3)
                sc, dc = cols_for(dy)
                first.append(push(src.at[sr, sc], dst.at[dr, dc], at(dx, dy)))

    for k in (2, 4, 5):
        loads[k].wait()
    lane8 = lax.broadcasted_iota(jnp.int32, (8, LANES), 1)
    lane1 = lax.broadcasted_iota(jnp.int32, (1, LANES), 1)

    def face_row(i, _):
        vec = jnp.zeros((1, LANES), jnp.int32)
        for jb in range(16):
            seg = ids[i, jb]
            value = tc[seg]
            cols = pl.ds(SIDE + 8 * jb, 8)
            G[DEPTH + i, cols, :] = G[DEPTH + i, cols, :] + jnp.where(lane8 == 0, value, 0.0)
            vec = jnp.where(lane1 // 8 == jb, seg, vec)
        idrow[i, :, :] = vec
        return 0

    lax.fori_loop(0, ROWS, face_row, 0)

    for dy in (1, -1):
        sc, dc = cols_for(dy)
        src_cols = pl.ds(SIDE + sc.start, sc.size)
        near.append(push(G.at[OWN_ROWS, src_cols], G.at[OWN_ROWS, dc], at(0, dy)))
    for dx in (1, -1):
        sr, dr = rows_for(dx, 1, 1)
        first.append(push(G.at[pl.ds(DEPTH + sr.start, 1), OWN_COLS], G.at[dr, OWN_COLS], at(dx, 0)))
    for dx in (1, -1):
        for dy in (1, -1):
            sr, dr = rows_for(dx, 1, 2)
            sc, dc = cols_for(dy)
            first.append(
                push(
                    G.at[pl.ds(DEPTH + sr.start, 2), pl.ds(SIDE + sc.start, SIDE)],
                    G.at[dr, dc],
                    at(dx, dy),
                )
            )
    for src, dst in pairs:
        for dx in (1, -1):
            sr, dr = rows_for(dx, 3, 1)
            second.append(push(src.at[sr], dst.at[dr, OWN_COLS], at(dx, 0)))
    for dx in (1, -1):
        sr, dr = rows_for(dx, 2, 1)
        second.append(push(G.at[pl.ds(DEPTH + sr.start, 1), OWN_COLS], G.at[dr, OWN_COLS], at(dx, 0)))

    col = lax.broadcasted_iota(jnp.int32, (WIDE, LANES), 0)
    lane = lax.broadcasted_iota(jnp.int32, (WIDE, LANES), 1)
    left_edge = jnp.logical_and(col == SIDE, gy == 0)
    right_edge = jnp.logical_and(col == SIDE + COLS - 1, gy == ny - 1)

    def setup(r):
        centre = C[r]
        up = jnp.where(jnp.logical_and(r == DEPTH + ROWS - 1, gx == nx - 1), 0.0, C[r + 1])
        down = jnp.where(jnp.logical_and(r == DEPTH, gx == 0), 0.0, C[r - 1])
        right = jnp.where(right_edge, 0.0, pltpu.roll(centre, WIDE - 1, 0))
        left = jnp.where(left_edge, 0.0, pltpu.roll(centre, 1, 0))
        above = jnp.where(lane == LANES - 1, 0.0, pltpu.roll(centre, LANES - 1, 1))
        below = jnp.where(lane == 0, 0.0, pltpu.roll(centre, 1, 1))
        DG[r] = G[r] + (3.0 * centre + 0.5 * ((up + down) + (right + left) + (above + below)))
        WYp[r] = jnp.where(right_edge, 0.0, 0.5 * (centre + right))
        WYm[r] = jnp.where(left_edge, 0.0, 0.5 * (centre + left))
        WZp[r] = jnp.where(lane == LANES - 1, 0.0, 0.5 * (centre + above))
        WZm[r] = jnp.where(lane == 0, 0.0, 0.5 * (centre + below))
        outer = jnp.logical_or(
            jnp.logical_and(r == DEPTH + ROWS - 1, gx == nx - 1), jnp.logical_and(r == DEPTH - 1, gx == 0)
        )
        WX[r] = jnp.where(outer, 0.0, 0.5 * (centre + up))

    def setup_low(r):
        centre = C[r]
        WX[r - 1] = jnp.where(jnp.logical_and(r == DEPTH, gx == 0), 0.0, 0.5 * (centre + C[r - 1]))

    def step(n, r):
        a, beta = COEF[n - 1]
        src = B if n == 1 else X.at[n - 2]
        x = src[r]
        acc = WX[r] * src[r + 1] + WX[r - 1] * src[r - 1]
        acc += WYp[r] * pltpu.roll(x, WIDE - 1, 0) + WYm[r] * pltpu.roll(x, 1, 0)
        acc += WZp[r] * pltpu.roll(x, LANES - 1, 1) + WZm[r] * pltpu.roll(x, 1, 1)
        acc = acc - DG[r] * x
        if n == 1:
            return ((1.0 + a) / THETA + beta) * x + (beta / THETA) * acc
        b = B[r]
        if n == 2:
            return (1.0 + a) * x + (beta - a / THETA) * b + beta * acc
        return (1.0 + a) * x - a * X[n - 3, r] + beta * (b + acc)

    def run(n, rows):
        for i in rows:
            new = step(n, i + DEPTH)
            if n < ITERS - 1:
                X[n - 1, i + DEPTH] = new
            else:
                own = new[SIDE : SIDE + COLS]
                out[i] = own
                acc = jnp.zeros((8, LANES), F32)
                for jb in range(16):
                    piece = jnp.where(lane8 == 0, own[8 * jb : 8 * jb + 8], 0.0)
                    acc = acc + pltpu.roll(piece, 8 * jb, 1, stride=1, stride_axis=0)
                face[i] = jnp.sum(acc, axis=0, keepdims=True) * gap[i : i + 1, :]

    x_copies = {}

    def send_x(n):
        for side, dx, src_row, dst_row in ((0, 1, 5, 0), (1, -1, 2, TALL - 1)):
            cp = pltpu.make_async_remote_copy(
                X.at[n - 2, DEPTH + src_row], X.at[n - 2, dst_row],
                x_send.at[side, n - 2], x_recv.at[side, n - 2],
                device_id=at(dx, 0), device_id_type=MESH,
            )
            cp.start()
            x_copies[side, n] = cp

    loads[0].wait()
    loads[1].wait()
    loads[3].wait()
    for cp in near:
        cp.wait_recv()
    setup_low(1 + DEPTH)
    for i in range(1, 7):
        setup(i + DEPTH)
    run(1, range(1, 7))
    send_x(2)
    run(2, range(2, 6))
    send_x(3)
    run(3, (3, 4))

    sub128 = lax.broadcasted_iota(jnp.int32, (LANES, LANES), 0)

    def one_hot(i, _):
        seg = idrow[i]
        low = ((seg >> 5) & 15) * 8 + (seg & 7)
        hot[i] = jnp.where(sub128 == low, 1.0, 0.0).astype(jnp.bfloat16)
        return 0

    lax.fori_loop(0, ROWS, one_hot, 0)

    for cp in first:
        cp.wait_recv()
    setup_low(-1 + DEPTH)
    for i in (-1, 0, 7, 8):
        setup(i + DEPTH)
    run(1, (-1, 0, 7, 8))
    run(2, (0, 1, 6, 7))
    run(3, (1, 2, 5, 6))
    send_x(4)
    run(4, (2, 3, 4, 5))
    send_x(5)
    run(5, (3, 4))

    for cp in second:
        cp.wait_recv()
    setup_low(-2 + DEPTH)
    for i in (-2, 9):
        setup(i + DEPTH)
    run(1, (-2, 9))
    run(2, (-1, 8))
    run(3, (0, 7))
    run(4, (1, 6))
    run(5, (2, 5))
    run(6, (3, 4))

    for n in (2, 3):
        for side in (0, 1):
            x_copies[side, n].wait_recv()
    run(2, (-2, 9))
    run(3, (-2, -1, 8, 9))
    run(4, (-1, 0, 7, 8))
    run(5, (0, 1, 6, 7))
    run(6, (1, 2, 5, 6))
    run(7, (2, 3, 4, 5))

    for side in (0, 1):
        x_copies[side, 4].wait_recv()
    run(4, (-2, 9))
    run(5, (-1, 8))
    run(6, (0, 7))
    run(7, (1, 6))

    for side in (0, 1):
        x_copies[side, 5].wait_recv()
    run(5, (-2, 9))
    run(6, (-1, 8))
    run(7, (0, 7))

    sub16 = lax.broadcasted_iota(jnp.int32, (16, LANES), 0)
    total = jnp.zeros((48, LANES), F32)
    for i in range(ROWS):
        seg = idrow[i]
        high = (seg >> 9) * 4 + ((seg >> 3) & 3)
        value = jnp.where(sub16 == high, face[i], 0.0)
        v1 = value.astype(jnp.bfloat16).astype(F32)
        v2 = (value - v1).astype(jnp.bfloat16).astype(F32)
        v3 = value - v1 - v2
        left = jnp.concatenate([v1, v2, v3], axis=0).astype(jnp.bfloat16)
        total = total + lax.dot_general(
            left, hot[i], (((1,), (1,)), ((), ())), preferred_element_type=F32
        )
    sums = total[0:16] + total[16:32] + total[32:48]
    for h in range(16):
        part[h] = sums[h : h + 1, :]

    copies = []
    for h in range(1, 16):
        dev = plane(h)
        row = (dev[0] // 16) * 4 + dev[1]
        cp = pltpu.make_async_remote_copy(
            part.at[row], got1.at[h], r_send.at[0, h], r_recv.at[0, h], device_id=dev, device_id_type=MESH
        )
        cp.start()
        copies.append(cp)
    acc = part[my_y * 4 + gy]
    for h, cp in enumerate(copies, 1):
        cp.wait_recv()
        acc = acc + got1[h]
    row2[...] = acc
    more = []
    for h in range(1, 16):
        cp = pltpu.make_async_remote_copy(
            row2, got2.at[h], r_send.at[1, h], r_recv.at[1, h], device_id=column(h), device_id_type=MESH
        )
        cp.start()
        more.append(cp)
    for h, cp in enumerate(more, 1):
        cp.wait_recv()
        acc = acc + got2[h]
    place = (my_z * 2 + my_c) * 8
    spread = jnp.broadcast_to(acc, (8, LANES))
    grad[...] = -pltpu.roll(spread, lax.rem(LANES - place, LANES), 1)

    for cp in sends + list(x_copies.values()) + copies + more:
        cp.wait_send()


def body(cot, cap, cond, gap, tc, ids):
    wide = pltpu.VMEM((TALL, WIDE, LANES), F32)
    n_static = 8 + 8 + 4 + 2 + 2 + 4 + 4 + 2
    adjoint, grad = pl.pallas_call(
        kernel,
        out_shape=(
            jax.ShapeDtypeStruct((ROWS, COLS, LANES), F32),
            jax.ShapeDtypeStruct((8, LANES), F32),
        ),
        in_specs=[pl.BlockSpec(memory_space=pltpu.HBM)] * 6,
        out_specs=(pl.BlockSpec(memory_space=pltpu.VMEM), pl.BlockSpec(memory_space=pltpu.VMEM)),
        scratch_shapes=[wide] * 9
        + [
            pltpu.VMEM((ITERS - 2, TALL, WIDE, LANES), F32),
            pltpu.VMEM((ROWS, COLS), F32),
            pltpu.SMEM((2048,), F32),
            pltpu.SMEM((ROWS, 16), jnp.int32),
            pltpu.VMEM((ROWS, LANES, LANES), jnp.bfloat16),
            pltpu.VMEM((ROWS, 1, LANES), jnp.int32),
            pltpu.VMEM((ROWS, 1, LANES), F32),
            pltpu.VMEM((16, 1, LANES), F32),
            pltpu.VMEM((16, 1, LANES), F32),
            pltpu.VMEM((1, LANES), F32),
            pltpu.VMEM((16, 1, LANES), F32),
            pltpu.SemaphoreType.DMA((6,)),
            pltpu.SemaphoreType.DMA((n_static,)),
            pltpu.SemaphoreType.DMA((n_static,)),
            pltpu.SemaphoreType.DMA((2, 4)),
            pltpu.SemaphoreType.DMA((2, 4)),
            pltpu.SemaphoreType.DMA((2, 16)),
            pltpu.SemaphoreType.DMA((2, 16)),
        ],
        compiler_params=pltpu.CompilerParams(
            collective_id=0, has_side_effects=True, vmem_limit_bytes=48 * 1024 * 1024
        ),
    )(*(pltpu.with_memory_space_constraint(v, pltpu.HBM) for v in (cot, cap, cond, gap, tc, ids)))
    return adjoint, grad[0, 0:8]


def solution(mesh):
    in_specs = (
        P("gx", "gy", None),
        P("gx", "gy", None),
        P("gx", "gy", None),
        P("gx", "gy"),
        P(),
        P("gx", "gy"),
    )
    out_specs = (P("gx", "gy", None), P(("gx", "gy")))
    return jax.shard_map(body, mesh=mesh, in_specs=in_specs, out_specs=out_specs, check_vma=False)
```

```python
import functools

import jax
import jax.numpy as jnp
from jax import lax
from jax.experimental import pallas as pl
from jax.experimental.pallas import tpu as pltpu
from jax.sharding import PartitionSpec as P

MESH = pl.DeviceIdType.MESH
F32 = jnp.float32
ITERS = 8
LOW_BOUND = 0.2
HIGH_BOUND = 28.0
THETA = (HIGH_BOUND + LOW_BOUND) / 2.0
DELTA = (HIGH_BOUND - LOW_BOUND) / 2.0
SIGMA = THETA / DELTA

ROWS, COLS, LANES = 8, 128, 128
DEPTH = 3
SIDE = 8
WIDE = COLS + 2 * SIDE
TALL = ROWS + 2 * DEPTH
REACH = ITERS - 1
SLAB = ROWS + 2 * REACH
OWN_ROWS = pl.ds(DEPTH, ROWS)
OWN_COLS = pl.ds(SIDE, COLS)


def coefficients():
    ratio = 1.0 / SIGMA
    out = []
    for _ in range(ITERS - 1):
        new = 1.0 / (2.0 * SIGMA - ratio)
        out.append((new * ratio, 2.0 * new / DELTA))
        ratio = new
    return out


COEF = coefficients()


def kernel(
    cot, cap, cond, gap_in, tc_in, ids_in,
    out, grad,
    B, C, G, DG, WX, WYp, WYm, WZp, WZm, X, gap, tc, ids, hot, idrow, spread, part, got1, row2, got2,
    SP, SF, ES, ER, SX,
    loc_sem, st_send, st_recv, x_send, x_recv, r_send, r_recv,
):
    gx, gy = lax.axis_index("gx"), lax.axis_index("gy")
    nx, ny = 64, 4
    my_y, my_z, my_c = gx // 16, lax.rem(gx // 2, 8), lax.rem(gx, 2)

    def at(dx, dy):
        return (lax.rem(gx + dx + nx, nx), lax.rem(gy + dy + ny, ny))

    def plane(h):
        return (lax.rem(my_y + h // 4, 4) * 16 + my_z * 2 + my_c, lax.rem(gy + h % 4, 4))

    def column(h):
        return (my_y * 16 + lax.rem(my_z + h // 2, 8) * 2 + lax.rem(my_c + h % 2, 2), gy)

    barrier = pltpu.get_barrier_semaphore()
    around = [(dx, dy) for dx in (-1, 0, 1) for dy in (-1, 0, 1) if dx or dy]
    partners = [at(*d) for d in around] + [plane(h) for h in range(1, 16)] + [column(h) for h in range(1, 16)]
    for dev in partners:
        pl.semaphore_signal(barrier, inc=1, device_id=dev, device_id_type=MESH)

    loads = [
        pltpu.make_async_copy(cot, B.at[OWN_ROWS, OWN_COLS], loc_sem.at[0]),
        pltpu.make_async_copy(cond, C.at[OWN_ROWS, OWN_COLS], loc_sem.at[1]),
        pltpu.make_async_copy(cap, G.at[OWN_ROWS, OWN_COLS], loc_sem.at[2]),
        pltpu.make_async_copy(gap_in, gap, loc_sem.at[3]),
        pltpu.make_async_copy(tc_in, tc, loc_sem.at[4]),
        pltpu.make_async_copy(ids_in, ids, loc_sem.at[5]),
    ]
    for cp in loads:
        cp.start()

    sends = []
    counter = [0]

    def push(src, dst, dev):
        k = counter[0]
        counter[0] += 1
        cp = pltpu.make_async_remote_copy(
            src, dst, st_send.at[k], st_recv.at[k], device_id=dev, device_id_type=MESH
        )
        cp.start()
        sends.append(cp)
        return cp

    def rows_for(dx, depth_from, count):
        if dx > 0:
            first = ROWS - (depth_from + count - 1)
            return pl.ds(first, count), pl.ds(DEPTH - (depth_from + count - 1), count)
        return pl.ds(depth_from - 1, count), pl.ds(DEPTH + ROWS + depth_from - 1, count)

    def cols_for(dy):
        if dy > 0:
            return pl.ds(COLS - SIDE, SIDE), pl.ds(0, SIDE)
        if dy < 0:
            return pl.ds(0, SIDE), pl.ds(SIDE + COLS, SIDE)
        return pl.ds(0, COLS), OWN_COLS

    for k in (0, 1, 2, 4, 5):
        loads[k].wait()
    lane8 = lax.broadcasted_iota(jnp.int32, (8, LANES), 1)
    lane1 = lax.broadcasted_iota(jnp.int32, (1, LANES), 1)

    def face_row(i, _):
        vec = jnp.zeros((1, LANES), jnp.int32)
        for jb in range(16):
            seg = ids[i, jb]
            value = tc[seg]
            cols = pl.ds(SIDE + 8 * jb, 8)
            G[DEPTH + i, cols, :] = G[DEPTH + i, cols, :] + jnp.where(lane8 == 0, value, 0.0)
            vec = jnp.where(lane1 == REACH * (jb + 1), seg, vec)
        idrow[i, :, :] = vec
        return 0

    lax.fori_loop(0, ROWS, face_row, 0)

    sub8 = lax.broadcasted_iota(jnp.int32, (8, LANES), 0)
    height = lax.rem(lane8, REACH)
    low, top = height == 0, height == REACH - 1

    def pack_row(i, _):
        b = c = g = b7 = c7 = jnp.zeros((8, LANES), F32)
        for jb in range(16):
            cols = pl.ds(SIDE + 8 * jb, 8)
            at0 = REACH * (jb + 1)
            here = jnp.logical_and(lane8 >= at0, lane8 < at0 + REACH)
            over = lane8 == at0 + REACH
            vb = pltpu.roll(B[DEPTH + i, cols, :], at0, 1)
            vc = pltpu.roll(C[DEPTH + i, cols, :], at0, 1)
            vg = pltpu.roll(G[DEPTH + i, cols, :], at0, 1)
            b, c, g = jnp.where(here, vb, b), jnp.where(here, vc, c), jnp.where(here, vg, g)
            b7, c7 = jnp.where(over, vb, b7), jnp.where(over, vc, c7)
        b7, c7 = pltpu.roll(b7, LANES - 1, 1), pltpu.roll(c7, LANES - 1, 1)
        above = jnp.where(top, c7, pltpu.roll(c, LANES - 1, 1))
        below = jnp.where(low, 0.0, pltpu.roll(c, 1, 1))
        SP[REACH + i, 0] = b
        SP[REACH + i, 1] = c
        SP[REACH + i, 2] = g + c + 0.5 * (above + below)
        SP[REACH + i, 3] = jnp.where(top, 0.5 * (c + c7) * b7, 0.0)
        return 0

    lax.fori_loop(0, ROWS, pack_row, 0)
    lane4 = lax.broadcasted_iota(jnp.int32, (4, 8, LANES), 2)
    for side, block in ((0, 16), (1, 1)):
        acc = jnp.zeros((4, 8, LANES), F32)
        for r in range(ROWS):
            moved = pltpu.roll(SP[REACH + r], (REACH * (r - block)) % LANES, 2)
            acc = jnp.where(jnp.logical_and(lane4 >= REACH * r, lane4 < REACH * (r + 1)), moved, acc)
        ES[side] = acc

    pl.semaphore_wait(barrier, len(partners))

    layer = []
    for dx in (1, -1):
        src0, dst0 = (1, 0) if dx > 0 else (0, REACH + ROWS)
        layer.append(push(SP.at[pl.ds(REACH + src0, REACH)], SP.at[pl.ds(dst0, REACH)], at(dx, 0)))
    for side, dy in ((0, 1), (1, -1)):
        for dx in (1, -1, 0):
            layer.append(push(ES.at[side], ER.at[side, dx + 1], at(dx, dy)))

    near, first, second = [], [], []
    pairs = ((cot, B), (cond, C))
    for src, dst in pairs:
        for dy in (1, -1):
            sc, dc = cols_for(dy)
            near.append(push(src.at[:, sc], dst.at[OWN_ROWS, dc], at(0, dy)))
    for src, dst in pairs:
        for dx in (1, -1):
            sr, dr = rows_for(dx, 1, 2)
            first.append(push(src.at[sr], dst.at[dr, OWN_COLS], at(dx, 0)))
    for src, dst in pairs:
        for dx in (1, -1):
            for dy in (1, -1):
                sr, dr = rows_for(dx, 1, 3)
                sc, dc = cols_for(dy)
                first.append(push(src.at[sr, sc], dst.at[dr, dc], at(dx, dy)))

    for dy in (1, -1):
        sc, dc = cols_for(dy)
        src_cols = pl.ds(SIDE + sc.start, sc.size)
        near.append(push(G.at[OWN_ROWS, src_cols], G.at[OWN_ROWS, dc], at(0, dy)))
    for dx in (1, -1):
        sr, dr = rows_for(dx, 1, 1)
        first.append(push(G.at[pl.ds(DEPTH + sr.start, 1), OWN_COLS], G.at[dr, OWN_COLS], at(dx, 0)))
    for dx in (1, -1):
        for dy in (1, -1):
            sr, dr = rows_for(dx, 1, 2)
            sc, dc = cols_for(dy)
            first.append(
                push(
                    G.at[pl.ds(DEPTH + sr.start, 2), pl.ds(SIDE + sc.start, SIDE)],
                    G.at[dr, dc],
                    at(dx, dy),
                )
            )
    for src, dst in pairs:
        for dx in (1, -1):
            sr, dr = rows_for(dx, 3, 1)
            second.append(push(src.at[sr], dst.at[dr, OWN_COLS], at(dx, 0)))
    for dx in (1, -1):
        sr, dr = rows_for(dx, 2, 1)
        second.append(push(G.at[pl.ds(DEPTH + sr.start, 1), OWN_COLS], G.at[dr, OWN_COLS], at(dx, 0)))

    col = lax.broadcasted_iota(jnp.int32, (WIDE, LANES), 0)
    lane = lax.broadcasted_iota(jnp.int32, (WIDE, LANES), 1)
    left_edge = jnp.logical_and(col == SIDE, gy == 0)
    right_edge = jnp.logical_and(col == SIDE + COLS - 1, gy == ny - 1)

    def setup(r):
        centre = C[r]
        up = jnp.where(jnp.logical_and(r == DEPTH + ROWS - 1, gx == nx - 1), 0.0, C[r + 1])
        down = jnp.where(jnp.logical_and(r == DEPTH, gx == 0), 0.0, C[r - 1])
        right = jnp.where(right_edge, 0.0, pltpu.roll(centre, WIDE - 1, 0))
        left = jnp.where(left_edge, 0.0, pltpu.roll(centre, 1, 0))
        above = jnp.where(lane == LANES - 1, 0.0, pltpu.roll(centre, LANES - 1, 1))
        below = jnp.where(lane == 0, 0.0, pltpu.roll(centre, 1, 1))
        DG[r] = G[r] + (3.0 * centre + 0.5 * ((up + down) + (right + left) + (above + below)))
        WYp[r] = jnp.where(right_edge, 0.0, 0.5 * (centre + right))
        WYm[r] = jnp.where(left_edge, 0.0, 0.5 * (centre + left))
        WZp[r] = jnp.where(lane == LANES - 1, 0.0, 0.5 * (centre + above))
        WZm[r] = jnp.where(lane == 0, 0.0, 0.5 * (centre + below))
        outer = jnp.logical_or(
            jnp.logical_and(r == DEPTH + ROWS - 1, gx == nx - 1), jnp.logical_and(r == DEPTH - 1, gx == 0)
        )
        WX[r] = jnp.where(outer, 0.0, 0.5 * (centre + up))

    def setup_low(r):
        centre = C[r]
        WX[r - 1] = jnp.where(jnp.logical_and(r == DEPTH, gx == 0), 0.0, 0.5 * (centre + C[r - 1]))

    def step(n, r):
        a, beta = COEF[n - 1]
        src = B if n == 1 else X.at[n - 2]
        x = src[r]
        acc = WX[r] * src[r + 1] + WX[r - 1] * src[r - 1]
        acc += WYp[r] * pltpu.roll(x, WIDE - 1, 0) + WYm[r] * pltpu.roll(x, 1, 0)
        acc += WZp[r] * pltpu.roll(x, LANES - 1, 1) + WZm[r] * pltpu.roll(x, 1, 1)
        acc = acc - DG[r] * x
        if n == 1:
            return ((1.0 + a) / THETA + beta) * x + (beta / THETA) * acc
        b = B[r]
        if n == 2:
            return (1.0 + a) * x + (beta - a / THETA) * b + beta * acc
        return (1.0 + a) * x - a * X[n - 3, r] + beta * (b + acc)

    def run(n, rows):
        for i in rows:
            new = step(n, i + DEPTH)
            if n < ITERS - 1:
                X[n - 1, i + DEPTH] = new
            else:
                out[i] = new[SIDE : SIDE + COLS]

    x_copies = {}

    def send_x(n):
        for side, dx, src_row, dst_row in ((0, 1, 5, 0), (1, -1, 2, TALL - 1)):
            cp = pltpu.make_async_remote_copy(
                X.at[n - 2, DEPTH + src_row], X.at[n - 2, dst_row],
                x_send.at[side, n - 2], x_recv.at[side, n - 2],
                device_id=at(dx, 0), device_id_type=MESH,
            )
            cp.start()
            x_copies[side, n] = cp

    loads[3].wait()
    pick = [jnp.where(lax.rem(lane8, 8) == sub8, gap[i : i + 1, :], 0.0) for i in range(ROWS)]
    target = (lax.broadcasted_iota(jnp.int32, (LANES, LANES), 0) // 8 + 1) * REACH
    place = jnp.where(lax.broadcasted_iota(jnp.int32, (LANES, LANES), 1) == target, 1.0, 0.0).astype(jnp.bfloat16)

    def thirds(value):
        v1 = value.astype(jnp.bfloat16).astype(F32)
        v2 = (value - v1).astype(jnp.bfloat16).astype(F32)
        return jnp.concatenate([v1, v2, value - v1 - v2], axis=0).astype(jnp.bfloat16)

    laid = jnp.dot(thirds(jnp.concatenate(pick, axis=0)), place, preferred_element_type=F32)
    laid = laid[0:64] + laid[64:128] + laid[128:192]
    for i in range(ROWS):
        spread[i] = laid[8 * i : 8 * i + 8, :]

    sub128 = lax.broadcasted_iota(jnp.int32, (LANES, LANES), 0)

    def one_hot(i, _):
        seg = idrow[i]
        low = ((seg >> 5) & 15) * 8 + (seg & 7)
        hot[i] = jnp.where(sub128 == low, 1.0, 0.0).astype(jnp.bfloat16)
        return 0

    lax.fori_loop(0, ROWS, one_hot, 0)

    for cp in layer:
        cp.wait_recv()
    head, tail = lane4 < REACH, jnp.logical_and(lane4 >= 17 * REACH, lane4 < 18 * REACH)
    for dx in (-1, 0, 1):
        for r in range(ROWS):
            q = REACH + r - ROWS * dx
            if 0 <= q < SLAB:
                left = pltpu.roll(ER[0, dx + 1], (-REACH * r) % LANES, 2)
                right = pltpu.roll(ER[1, dx + 1], (REACH * (17 - r)) % LANES, 2)
                SF[q] = jnp.where(head, left, jnp.where(tail, right, SP[q]))

    def next_col(v):
        t = pltpu.roll(v, 7, 1)
        return jnp.where(lax.broadcasted_iota(jnp.int32, v.shape, 1) == 7, pltpu.roll(t, LANES - REACH, 2), t)

    def last_col(v):
        t = pltpu.roll(v, 1, 1)
        return jnp.where(lax.broadcasted_iota(jnp.int32, v.shape, 1) == 0, pltpu.roll(t, REACH, 2), t)

    def in_block(shape, block):
        spot = lax.broadcasted_iota(jnp.int32, shape, 2)
        return jnp.logical_and(spot >= REACH * block, spot < REACH * (block + 1))

    mid = (SLAB - 2, 8, LANES)
    rows_ = lax.broadcasted_iota(jnp.int32, mid, 0) + 1
    subs_ = lax.broadcasted_iota(jnp.int32, mid, 1)
    high_ = lax.rem(lax.broadcasted_iota(jnp.int32, mid, 2), REACH)
    off_up = jnp.logical_and(rows_ == REACH + ROWS - 1, gx == nx - 1)
    off_down = jnp.logical_and(rows_ == REACH, gx == 0)
    off_right = jnp.logical_and(jnp.logical_and(in_block(mid, 16), subs_ == 7), gy == ny - 1)
    off_left = jnp.logical_and(jnp.logical_and(in_block(mid, 1), subs_ == 0), gy == 0)
    sc_ = SF[1 : SLAB - 1, 1]
    near_cond = [
        jnp.where(off_up, 0.0, SF[2:SLAB, 1]),
        jnp.where(off_down, 0.0, SF[0 : SLAB - 2, 1]),
        jnp.where(off_right, 0.0, next_col(sc_)),
        jnp.where(off_left, 0.0, last_col(sc_)),
    ]
    diag_ = SF[1 : SLAB - 1, 2] + 2.0 * sc_
    weight = []
    for off, other in zip((off_up, off_down, off_right, off_left), near_cond):
        diag_ = diag_ + 0.5 * other
        weight.append(jnp.where(off, 0.0, 0.5 * (sc_ + other)))
    weight.append(jnp.where(high_ == REACH - 1, 0.0, 0.5 * (sc_ + pltpu.roll(sc_, LANES - 1, 2))))
    weight.append(jnp.where(high_ == 0, 0.0, 0.5 * (sc_ + pltpu.roll(sc_, 1, 2))))
    for k, w in enumerate(weight):
        SX[k, 1 : SLAB - 1] = w
    SX[6, 1 : SLAB - 1] = diag_

    for n in range(1, ITERS):
        a, beta = COEF[n - 1]
        lo, hi = n, SLAB - n

        def state(m, p, q):
            return SF[p:q, 0] if m == 1 else SX[5 + m, p:q]

        x = state(n, lo, hi)
        acc = SX[0, lo:hi] * state(n, lo + 1, hi + 1) + SX[1, lo:hi] * state(n, lo - 1, hi - 1)
        acc += SX[2, lo:hi] * next_col(x) + SX[3, lo:hi] * last_col(x)
        acc += SX[4, lo:hi] * pltpu.roll(x, LANES - 1, 2) + SX[5, lo:hi] * pltpu.roll(x, 1, 2)
        acc = acc - SX[6, lo:hi] * x
        b = SF[lo:hi, 0]
        if n == 1:
            new = ((1.0 + a) / THETA + beta) * x + (beta / THETA) * (acc + SF[lo:hi, 3])
        elif n == 2:
            new = (1.0 + a) * x + (beta - a / THETA) * b + beta * acc
        else:
            new = (1.0 + a) * x - a * state(n - 1, lo, hi) + beta * (b + acc)
        if n < ITERS - 1:
            SX[6 + n, lo:hi] = new
    faces = jnp.sum(new * spread[...], axis=1, keepdims=True)

    sub16 = lax.broadcasted_iota(jnp.int32, (16, LANES), 0)
    total = jnp.zeros((48, LANES), F32)
    for i in range(ROWS):
        seg = idrow[i]
        high = (seg >> 9) * 4 + ((seg >> 3) & 3)
        value = jnp.where(sub16 == high, faces[i], 0.0)
        left = thirds(value)
        total = total + lax.dot_general(
            left, hot[i], (((1,), (1,)), ((), ())), preferred_element_type=F32
        )
    sums = total[0:16] + total[16:32] + total[32:48]
    for h in range(16):
        part[h] = sums[h : h + 1, :]

    copies = []
    for h in range(1, 16):
        dev = plane(h)
        row = (dev[0] // 16) * 4 + dev[1]
        cp = pltpu.make_async_remote_copy(
            part.at[row], got1.at[h], r_send.at[0, h], r_recv.at[0, h], device_id=dev, device_id_type=MESH
        )
        cp.start()
        copies.append(cp)
    for cp in near:
        cp.wait_recv()
    setup_low(1 + DEPTH)
    for i in range(1, 7):
        setup(i + DEPTH)
    run(1, range(1, 7))
    send_x(2)
    run(2, range(2, 6))
    send_x(3)
    run(3, (3, 4))

    for cp in first:
        cp.wait_recv()
    setup_low(-1 + DEPTH)
    for i in (-1, 0, 7, 8):
        setup(i + DEPTH)
    run(1, (-1, 0, 7, 8))
    run(2, (0, 1, 6, 7))
    run(3, (1, 2, 5, 6))
    send_x(4)
    run(4, (2, 3, 4, 5))
    send_x(5)
    run(5, (3, 4))

    for cp in second:
        cp.wait_recv()
    setup_low(-2 + DEPTH)
    for i in (-2, 9):
        setup(i + DEPTH)
    run(1, (-2, 9))
    run(2, (-1, 8))
    run(3, (0, 7))
    run(4, (1, 6))
    run(5, (2, 5))
    run(6, (3, 4))

    acc = part[my_y * 4 + gy]
    for h, cp in enumerate(copies, 1):
        cp.wait_recv()
        acc = acc + got1[h]
    row2[...] = acc
    more = []
    for h in range(1, 16):
        cp = pltpu.make_async_remote_copy(
            row2, got2.at[h], r_send.at[1, h], r_recv.at[1, h], device_id=column(h), device_id_type=MESH
        )
        cp.start()
        more.append(cp)

    for n in (2, 3):
        for side in (0, 1):
            x_copies[side, n].wait_recv()
    run(2, (-2, 9))
    run(3, (-2, -1, 8, 9))
    run(4, (-1, 0, 7, 8))
    run(5, (0, 1, 6, 7))
    run(6, (1, 2, 5, 6))
    run(7, (2, 3, 4, 5))

    for side in (0, 1):
        x_copies[side, 4].wait_recv()
    run(4, (-2, 9))
    run(5, (-1, 8))
    run(6, (0, 7))
    run(7, (1, 6))

    for side in (0, 1):
        x_copies[side, 5].wait_recv()
    run(5, (-2, 9))
    run(6, (-1, 8))
    run(7, (0, 7))

    acc = row2[...]
    for h, cp in enumerate(more, 1):
        cp.wait_recv()
        acc = acc + got2[h]
    owned = (my_z * 2 + my_c) * 8
    grad[...] = -pltpu.roll(jnp.broadcast_to(acc, (8, LANES)), lax.rem(LANES - owned, LANES), 1)

    for cp in sends + list(x_copies.values()) + copies + more:
        cp.wait_send()


def body(cot, cap, cond, gap, tc, ids):
    wide = pltpu.VMEM((TALL, WIDE, LANES), F32)
    n_static = 8 + 4 + 4 + 8 + 2 + 2 + 4 + 4 + 2
    adjoint, grad = pl.pallas_call(
        kernel,
        out_shape=(
            jax.ShapeDtypeStruct((ROWS, COLS, LANES), F32),
            jax.ShapeDtypeStruct((8, LANES), F32),
        ),
        in_specs=[pl.BlockSpec(memory_space=pltpu.HBM)] * 6,
        out_specs=(pl.BlockSpec(memory_space=pltpu.VMEM), pl.BlockSpec(memory_space=pltpu.VMEM)),
        scratch_shapes=[wide] * 9
        + [
            pltpu.VMEM((ITERS - 2, TALL, WIDE, LANES), F32),
            pltpu.VMEM((ROWS, COLS), F32),
            pltpu.SMEM((2048,), F32),
            pltpu.SMEM((ROWS, 16), jnp.int32),
            pltpu.VMEM((ROWS, LANES, LANES), jnp.bfloat16),
            pltpu.VMEM((ROWS, 1, LANES), jnp.int32),
            pltpu.VMEM((ROWS, 8, LANES), F32),
            pltpu.VMEM((16, 1, LANES), F32),
            pltpu.VMEM((16, 1, LANES), F32),
            pltpu.VMEM((1, LANES), F32),
            pltpu.VMEM((16, 1, LANES), F32),
            pltpu.VMEM((SLAB, 4, 8, LANES), F32),
            pltpu.VMEM((SLAB, 4, 8, LANES), F32),
            pltpu.VMEM((2, 4, 8, LANES), F32),
            pltpu.VMEM((2, 3, 4, 8, LANES), F32),
            pltpu.VMEM((13, SLAB, 8, LANES), F32),
            pltpu.SemaphoreType.DMA((6,)),
            pltpu.SemaphoreType.DMA((n_static,)),
            pltpu.SemaphoreType.DMA((n_static,)),
            pltpu.SemaphoreType.DMA((2, 4)),
            pltpu.SemaphoreType.DMA((2, 4)),
            pltpu.SemaphoreType.DMA((2, 16)),
            pltpu.SemaphoreType.DMA((2, 16)),
        ],
        compiler_params=pltpu.CompilerParams(
            collective_id=0, has_side_effects=True, vmem_limit_bytes=48 * 1024 * 1024
        ),
    )(*(pltpu.with_memory_space_constraint(v, pltpu.HBM) for v in (cot, cap, cond, gap, tc, ids)))
    return adjoint, grad[0, 0:8]


def solution(mesh):
    in_specs = (
        P("gx", "gy", None),
        P("gx", "gy", None),
        P("gx", "gy", None),
        P("gx", "gy"),
        P(),
        P("gx", "gy"),
    )
    out_specs = (P("gx", "gy", None), P(("gx", "gy")))
    return jax.shard_map(body, mesh=mesh, in_specs=in_specs, out_specs=out_specs, check_vma=False)
```

```python
import functools

import jax
import jax.numpy as jnp
from jax import lax
from jax.experimental import pallas as pl
from jax.experimental.pallas import tpu as pltpu
from jax.sharding import PartitionSpec as P

MESH = pl.DeviceIdType.MESH
F32 = jnp.float32
ITERS = 8
LOW_BOUND = 0.2
HIGH_BOUND = 28.0
THETA = (HIGH_BOUND + LOW_BOUND) / 2.0
DELTA = (HIGH_BOUND - LOW_BOUND) / 2.0
SIGMA = THETA / DELTA

ROWS, COLS, LANES = 8, 128, 128
DEPTH = 3
SIDE = 8
WIDE = COLS + 2 * SIDE
TALL = ROWS + 2 * DEPTH
REACH = ITERS - 1
SLAB = ROWS + 2 * REACH
OWN_ROWS = pl.ds(DEPTH, ROWS)
OWN_COLS = pl.ds(SIDE, COLS)


def coefficients():
    ratio = 1.0 / SIGMA
    out = []
    for _ in range(ITERS - 1):
        new = 1.0 / (2.0 * SIGMA - ratio)
        out.append((new * ratio, 2.0 * new / DELTA))
        ratio = new
    return out


COEF = coefficients()


def kernel(
    cot, cap, cond, gap_in, tc_in, ids_in,
    out, grad,
    B, C, G, DG, WX, WYp, WYm, WZp, WZm, X, gap, tc, ids, hot, idrow, spread, part, got1, row2, got2,
    SP, SF, SB, RB, ES, ER, SX,
    loc_sem, st_send, st_recv, x_send, x_recv, r_send, r_recv,
):
    gx, gy = lax.axis_index("gx"), lax.axis_index("gy")
    nx, ny = 64, 4
    my_y, my_z, my_c = gx // 16, lax.rem(gx // 2, 8), lax.rem(gx, 2)

    def at(dx, dy):
        return (lax.rem(gx + dx + nx, nx), lax.rem(gy + dy + ny, ny))

    def plane(h):
        return (lax.rem(my_y + h // 4, 4) * 16 + my_z * 2 + my_c, lax.rem(gy + h % 4, 4))

    def column(h):
        return (my_y * 16 + lax.rem(my_z + h // 2, 8) * 2 + lax.rem(my_c + h % 2, 2), gy)

    plane_order = sorted(range(1, 16), key=lambda h: -min(h // 4, 4 - h // 4) - min(h % 4, 4 - h % 4))
    column_order = sorted(range(1, 16), key=lambda h: -min(h // 2, 8 - h // 2) - (h % 2) / 2)

    barrier = pltpu.get_barrier_semaphore()
    around = [(dx, dy) for dx in (-1, 0, 1) for dy in (-1, 0, 1) if dx or dy]
    partners = [at(*d) for d in around] + [plane(h) for h in range(1, 16)] + [column(h) for h in range(1, 16)]
    for dev in partners:
        pl.semaphore_signal(barrier, inc=1, device_id=dev, device_id_type=MESH)

    loads = [
        pltpu.make_async_copy(cot, B.at[OWN_ROWS, OWN_COLS], loc_sem.at[0]),
        pltpu.make_async_copy(cond, C.at[OWN_ROWS, OWN_COLS], loc_sem.at[1]),
        pltpu.make_async_copy(cap, G.at[OWN_ROWS, OWN_COLS], loc_sem.at[2]),
        pltpu.make_async_copy(gap_in, gap, loc_sem.at[3]),
        pltpu.make_async_copy(tc_in, tc, loc_sem.at[4]),
        pltpu.make_async_copy(ids_in, ids, loc_sem.at[5]),
    ]
    for cp in loads:
        cp.start()

    sends = []
    counter = [0]

    def push(src, dst, dev):
        k = counter[0]
        counter[0] += 1
        cp = pltpu.make_async_remote_copy(
            src, dst, st_send.at[k], st_recv.at[k], device_id=dev, device_id_type=MESH
        )
        cp.start()
        sends.append(cp)
        return cp

    def rows_for(dx, depth_from, count):
        if dx > 0:
            first = ROWS - (depth_from + count - 1)
            return pl.ds(first, count), pl.ds(DEPTH - (depth_from + count - 1), count)
        return pl.ds(depth_from - 1, count), pl.ds(DEPTH + ROWS + depth_from - 1, count)

    def cols_for(dy):
        if dy > 0:
            return pl.ds(COLS - SIDE, SIDE), pl.ds(0, SIDE)
        if dy < 0:
            return pl.ds(0, SIDE), pl.ds(SIDE + COLS, SIDE)
        return pl.ds(0, COLS), OWN_COLS

    for k in (0, 1, 2, 4, 5):
        loads[k].wait()
    lane8 = lax.broadcasted_iota(jnp.int32, (8, LANES), 1)
    lane1 = lax.broadcasted_iota(jnp.int32, (1, LANES), 1)

    def face_row(i, _):
        vec = jnp.zeros((1, LANES), jnp.int32)
        for jb in range(16):
            seg = ids[i, jb]
            value = tc[seg]
            cols = pl.ds(SIDE + 8 * jb, 8)
            G[DEPTH + i, cols, :] = G[DEPTH + i, cols, :] + jnp.where(lane8 == 0, value, 0.0)
            vec = jnp.where(lane1 == REACH * (jb + 1), seg, vec)
        idrow[i, :, :] = vec
        return 0

    lax.fori_loop(0, ROWS, face_row, 0)

    sub8 = lax.broadcasted_iota(jnp.int32, (8, LANES), 0)
    height = lax.rem(lane8, REACH)
    low, top = height == 0, height == REACH - 1

    def pack_row(i, _):
        b = c = g = b7 = c7 = jnp.zeros((8, LANES), F32)
        for jb in range(16):
            cols = pl.ds(SIDE + 8 * jb, 8)
            at0 = REACH * (jb + 1)
            here = jnp.logical_and(lane8 >= at0, lane8 < at0 + REACH)
            over = lane8 == at0 + REACH
            vb = pltpu.roll(B[DEPTH + i, cols, :], at0, 1)
            vc = pltpu.roll(C[DEPTH + i, cols, :], at0, 1)
            vg = pltpu.roll(G[DEPTH + i, cols, :], at0, 1)
            b, c, g = jnp.where(here, vb, b), jnp.where(here, vc, c), jnp.where(here, vg, g)
            b7, c7 = jnp.where(over, vb, b7), jnp.where(over, vc, c7)
        b7, c7 = pltpu.roll(b7, LANES - 1, 1), pltpu.roll(c7, LANES - 1, 1)
        above = jnp.where(top, c7, pltpu.roll(c, LANES - 1, 1))
        below = jnp.where(low, 0.0, pltpu.roll(c, 1, 1))
        SP[i, 0] = b
        SP[i, 1] = c
        SP[i, 2] = g + c + 0.5 * (above + below)
        SP[i, 3] = jnp.where(top, 0.5 * (c + c7) * b7, 0.0)
        return 0

    lax.fori_loop(0, ROWS, pack_row, 0)
    for side, row0 in ((0, 1), (1, 0)):
        terms = jnp.zeros((8, LANES), F32)
        for k in range(REACH):
            for arr in range(3):
                SB[side, 3 * k + arr] = SP[row0 + k, arr]
            terms = jnp.where(height == k, pltpu.roll(SP[row0 + k, 3], (k - REACH + 1) % LANES, 1), terms)
        SB[side, 3 * REACH] = terms
    HALF = REACH * ROWS
    for side, block in ((0, 16), (1, 1)):
        tiles = [jnp.zeros((8, LANES), F32)] * 2
        for r in range(ROWS):
            for arr, tile, to, width in ((0, 0, REACH * r, REACH), (1, 0, HALF + REACH * r, REACH),
                                         (2, 1, REACH * r, REACH), (3, 1, HALF + r, 1)):
                start = REACH * block + (REACH - 1 if arr == 3 else 0)
                moved = pltpu.roll(SP[r, arr], (to - start) % LANES, 1)
                tiles[tile] = jnp.where(jnp.logical_and(lane8 >= to, lane8 < to + width), moved, tiles[tile])
        ES[side, 0], ES[side, 1] = tiles

    pl.semaphore_wait(barrier, len(partners))

    layer = []
    for dx in (1, -1):
        for side, dy in ((0, 1), (1, -1)):
            layer.append(push(ES.at[side], ER.at[side, dx + 1], at(dx, dy)))
    for side, dx in ((0, 1), (1, -1)):
        layer.append(push(SB.at[side], RB.at[side], at(dx, 0)))
    for side, dy in ((0, 1), (1, -1)):
        layer.append(push(ES.at[side], ER.at[side, 1], at(0, dy)))

    near, first, second = [], [], []
    pairs = ((cot, B), (cond, C))
    for src, dst in pairs:
        for dy in (1, -1):
            sc, dc = cols_for(dy)
            near.append(push(src.at[:, sc], dst.at[OWN_ROWS, dc], at(0, dy)))
    first2 = []
    for depth, group in ((1, first), (2, first2)):
        for src, dst in pairs:
            for dx in (1, -1):
                sr, dr = rows_for(dx, depth, 1)
                group.append(push(src.at[sr], dst.at[dr, OWN_COLS], at(dx, 0)))
    for src, dst in pairs:
        for dx in (1, -1):
            for dy in (1, -1):
                sr, dr = rows_for(dx, 1, 3)
                sc, dc = cols_for(dy)
                first.append(push(src.at[sr, sc], dst.at[dr, dc], at(dx, dy)))

    for dy in (1, -1):
        sc, dc = cols_for(dy)
        src_cols = pl.ds(SIDE + sc.start, sc.size)
        near.append(push(G.at[OWN_ROWS, src_cols], G.at[OWN_ROWS, dc], at(0, dy)))
    for dx in (1, -1):
        sr, dr = rows_for(dx, 1, 1)
        first2.append(push(G.at[pl.ds(DEPTH + sr.start, 1), OWN_COLS], G.at[dr, OWN_COLS], at(dx, 0)))
    for dx in (1, -1):
        for dy in (1, -1):
            sr, dr = rows_for(dx, 1, 2)
            sc, dc = cols_for(dy)
            first2.append(
                push(
                    G.at[pl.ds(DEPTH + sr.start, 2), pl.ds(SIDE + sc.start, SIDE)],
                    G.at[dr, dc],
                    at(dx, dy),
                )
            )
    for src, dst in pairs:
        for dx in (1, -1):
            sr, dr = rows_for(dx, 3, 1)
            second.append(push(src.at[sr], dst.at[dr, OWN_COLS], at(dx, 0)))
    for dx in (1, -1):
        sr, dr = rows_for(dx, 2, 1)
        second.append(push(G.at[pl.ds(DEPTH + sr.start, 1), OWN_COLS], G.at[dr, OWN_COLS], at(dx, 0)))

    inner = (SIDE, SIDE + COLS, SIDE + 8, SIDE + COLS - 8)
    inner2 = (SIDE + 8, SIDE + COLS - 8, SIDE + 16, SIDE + COLS - 16)
    rims = ((0, SIDE + 16, 0, SIDE + 8), (SIDE + COLS - 16, WIDE, SIDE + COLS - 8, WIDE))
    rims2 = ((0, SIDE + 24, 0, SIDE + 16), (SIDE + COLS - 24, WIDE, SIDE + COLS - 16, WIDE))

    def window(span):
        lo, hi, start, stop = span
        return pl.ds(lo, hi - lo), hi - lo, pl.ds(start, stop - start), lambda v: v[start - lo : stop - lo]

    def setup(r, span=(0, WIDE, 0, WIDE)):
        read, width, keep, cut = window(span)
        col = lax.broadcasted_iota(jnp.int32, (span[3] - span[2], LANES), 0) + span[2]
        lane = lax.broadcasted_iota(jnp.int32, (span[3] - span[2], LANES), 1)
        left_edge = jnp.logical_and(col == SIDE, gy == 0)
        right_edge = jnp.logical_and(col == SIDE + COLS - 1, gy == ny - 1)
        line = C[r, read, :]
        centre = cut(line)
        up = jnp.where(jnp.logical_and(r == DEPTH + ROWS - 1, gx == nx - 1), 0.0, C[r + 1, keep, :])
        down = jnp.where(jnp.logical_and(r == DEPTH, gx == 0), 0.0, C[r - 1, keep, :])
        right = jnp.where(right_edge, 0.0, cut(pltpu.roll(line, width - 1, 0)))
        left = jnp.where(left_edge, 0.0, cut(pltpu.roll(line, 1, 0)))
        above = jnp.where(lane == LANES - 1, 0.0, pltpu.roll(centre, LANES - 1, 1))
        below = jnp.where(lane == 0, 0.0, pltpu.roll(centre, 1, 1))
        DG[r, keep, :] = G[r, keep, :] + (
            3.0 * centre + 0.5 * ((up + down) + (right + left) + (above + below))
        )
        WYp[r, keep, :] = jnp.where(right_edge, 0.0, 0.5 * (centre + right))
        WYm[r, keep, :] = jnp.where(left_edge, 0.0, 0.5 * (centre + left))
        WZp[r, keep, :] = jnp.where(lane == LANES - 1, 0.0, 0.5 * (centre + above))
        WZm[r, keep, :] = jnp.where(lane == 0, 0.0, 0.5 * (centre + below))
        outer = jnp.logical_or(
            jnp.logical_and(r == DEPTH + ROWS - 1, gx == nx - 1), jnp.logical_and(r == DEPTH - 1, gx == 0)
        )
        WX[r, keep, :] = jnp.where(outer, 0.0, 0.5 * (centre + up))

    def setup_low(r, keep=pl.ds(0, WIDE)):
        WX[r - 1, keep, :] = jnp.where(
            jnp.logical_and(r == DEPTH, gx == 0), 0.0, 0.5 * (C[r, keep, :] + C[r - 1, keep, :])
        )

    def step(n, r, span):
        a, beta = COEF[n - 1]
        read, width, keep, cut = window(span)
        src = B if n == 1 else X.at[n - 2]
        line = src[r, read, :]
        x = cut(line)
        acc = WX[r, keep, :] * src[r + 1, keep, :] + WX[r - 1, keep, :] * src[r - 1, keep, :]
        acc += WYp[r, keep, :] * cut(pltpu.roll(line, width - 1, 0)) + WYm[r, keep, :] * cut(pltpu.roll(line, 1, 0))
        acc += WZp[r, keep, :] * pltpu.roll(x, LANES - 1, 1) + WZm[r, keep, :] * pltpu.roll(x, 1, 1)
        acc = acc - DG[r, keep, :] * x
        if n == 1:
            return ((1.0 + a) / THETA + beta) * x + (beta / THETA) * acc
        b = B[r, keep, :]
        if n == 2:
            return (1.0 + a) * x + (beta - a / THETA) * b + beta * acc
        return (1.0 + a) * x - a * X[n - 3, r, keep, :] + beta * (b + acc)

    def run(n, rows, span=(0, WIDE, 0, WIDE)):
        for i in rows:
            new = step(n, i + DEPTH, span)
            if n < ITERS - 1:
                X[n - 1, i + DEPTH, pl.ds(span[2], span[3] - span[2]), :] = new
            else:
                out[i] = new[SIDE : SIDE + COLS]

    x_copies = {}

    def send_x(n):
        for side, dx, src_row, dst_row in ((0, 1, 5, 0), (1, -1, 2, TALL - 1)):
            cp = pltpu.make_async_remote_copy(
                X.at[n - 2, DEPTH + src_row], X.at[n - 2, dst_row],
                x_send.at[side, n - 2], x_recv.at[side, n - 2],
                device_id=at(dx, 0), device_id_type=MESH,
            )
            cp.start()
            x_copies[side, n] = cp

    loads[3].wait()
    pick = [jnp.where(lax.rem(lane8, 8) == sub8, gap[i : i + 1, :], 0.0) for i in range(ROWS)]
    target = (lax.broadcasted_iota(jnp.int32, (LANES, LANES), 0) // 8 + 1) * REACH
    place = jnp.where(lax.broadcasted_iota(jnp.int32, (LANES, LANES), 1) == target, 1.0, 0.0).astype(jnp.bfloat16)

    def thirds(value):
        v1 = value.astype(jnp.bfloat16).astype(F32)
        v2 = (value - v1).astype(jnp.bfloat16).astype(F32)
        return jnp.concatenate([v1, v2, value - v1 - v2], axis=0).astype(jnp.bfloat16)

    laid = jnp.dot(thirds(jnp.concatenate(pick, axis=0)), place, preferred_element_type=F32)
    laid = laid[0:64] + laid[64:128] + laid[128:192]
    for i in range(ROWS):
        spread[i] = laid[8 * i : 8 * i + 8, :]

    sub128 = lax.broadcasted_iota(jnp.int32, (LANES, LANES), 0)

    def one_hot(i, _):
        seg = idrow[i]
        low = ((seg >> 5) & 15) * 8 + (seg & 7)
        hot[i] = jnp.where(sub128 == low, 1.0, 0.0).astype(jnp.bfloat16)
        return 0

    lax.fori_loop(0, ROWS, one_hot, 0)

    setup_low(1 + DEPTH, pl.ds(inner[2], inner[3] - inner[2]))
    for i in range(1, 7):
        setup(i + DEPTH, inner)
    run(1, range(1, 7), inner)
    run(2, range(2, 6), inner2)

    for cp in layer:
        cp.wait_recv()
    head = lane8 < REACH
    tail = jnp.logical_and(lane8 >= 17 * REACH, lane8 < 18 * REACH)
    for dx in (-1, 0, 1):
        for r in range(ROWS):
            q = REACH + r - ROWS * dx
            if not 0 <= q < SLAB:
                continue
            for arr, tile, start in ((0, 0, REACH * r), (1, 0, HALF + REACH * r), (2, 1, REACH * r), (3, 1, HALF + r)):
                skip = REACH - 1 if arr == 3 else 0
                if dx == 0:
                    own = SP[r, arr]
                elif arr < 3:
                    own = RB[0 if dx > 0 else 1, 3 * (r - (1 if dx > 0 else 0)) + arr]
                else:
                    k = r - (1 if dx > 0 else 0)
                    own = pltpu.roll(RB[0 if dx > 0 else 1, 3 * REACH], REACH - 1 - k, 1)
                left = pltpu.roll(ER[0, dx + 1, tile], (skip - start) % LANES, 1)
                right = pltpu.roll(ER[1, dx + 1, tile], (17 * REACH + skip - start) % LANES, 1)
                row = jnp.where(head, left, jnp.where(tail, right, own))
                SF[q, arr] = jnp.where(top, row, 0.0) if arr == 3 else row

    def next_col(v):
        t = pltpu.roll(v, 7, 1)
        return jnp.where(lax.broadcasted_iota(jnp.int32, v.shape, 1) == 7, pltpu.roll(t, LANES - REACH, 2), t)

    def last_col(v):
        t = pltpu.roll(v, 1, 1)
        return jnp.where(lax.broadcasted_iota(jnp.int32, v.shape, 1) == 0, pltpu.roll(t, REACH, 2), t)

    def in_block(shape, block):
        spot = lax.broadcasted_iota(jnp.int32, shape, 2)
        return jnp.logical_and(spot >= REACH * block, spot < REACH * (block + 1))

    mid = (SLAB - 2, 8, LANES)
    rows_ = lax.broadcasted_iota(jnp.int32, mid, 0) + 1
    subs_ = lax.broadcasted_iota(jnp.int32, mid, 1)
    high_ = lax.rem(lax.broadcasted_iota(jnp.int32, mid, 2), REACH)
    off_up = jnp.logical_and(rows_ == REACH + ROWS - 1, gx == nx - 1)
    off_down = jnp.logical_and(rows_ == REACH, gx == 0)
    off_right = jnp.logical_and(jnp.logical_and(in_block(mid, 16), subs_ == 7), gy == ny - 1)
    off_left = jnp.logical_and(jnp.logical_and(in_block(mid, 1), subs_ == 0), gy == 0)
    sc_ = SF[1 : SLAB - 1, 1]
    near_cond = [
        jnp.where(off_up, 0.0, SF[2:SLAB, 1]),
        jnp.where(off_down, 0.0, SF[0 : SLAB - 2, 1]),
        jnp.where(off_right, 0.0, next_col(sc_)),
        jnp.where(off_left, 0.0, last_col(sc_)),
    ]
    diag_ = SF[1 : SLAB - 1, 2] + 2.0 * sc_
    weight = []
    for off, other in zip((off_up, off_down, off_right, off_left), near_cond):
        diag_ = diag_ + 0.5 * other
        weight.append(jnp.where(off, 0.0, 0.5 * (sc_ + other)))
    weight.append(jnp.where(high_ == REACH - 1, 0.0, 0.5 * (sc_ + pltpu.roll(sc_, LANES - 1, 2))))
    weight.append(jnp.where(high_ == 0, 0.0, 0.5 * (sc_ + pltpu.roll(sc_, 1, 2))))
    for k, w in enumerate(weight):
        SX[k, 1 : SLAB - 1] = w
    SX[6, 1 : SLAB - 1] = diag_

    for n in range(1, ITERS):
        a, beta = COEF[n - 1]
        lo, hi = n, SLAB - n

        def state(m, p, q):
            return SF[p:q, 0] if m == 1 else SX[5 + m, p:q]

        x = state(n, lo, hi)
        acc = SX[0, lo:hi] * state(n, lo + 1, hi + 1) + SX[1, lo:hi] * state(n, lo - 1, hi - 1)
        acc += SX[2, lo:hi] * next_col(x) + SX[3, lo:hi] * last_col(x)
        acc += SX[4, lo:hi] * pltpu.roll(x, LANES - 1, 2) + SX[5, lo:hi] * pltpu.roll(x, 1, 2)
        acc = acc - SX[6, lo:hi] * x
        b = SF[lo:hi, 0]
        if n == 1:
            new = ((1.0 + a) / THETA + beta) * x + (beta / THETA) * (acc + SF[lo:hi, 3])
        elif n == 2:
            new = (1.0 + a) * x + (beta - a / THETA) * b + beta * acc
        else:
            new = (1.0 + a) * x - a * state(n - 1, lo, hi) + beta * (b + acc)
        if n < ITERS - 1:
            SX[6 + n, lo:hi] = new
    faces = jnp.sum(new * spread[...], axis=1, keepdims=True)

    sub16 = lax.broadcasted_iota(jnp.int32, (16, LANES), 0)
    total = jnp.zeros((48, LANES), F32)
    for i in range(ROWS):
        seg = idrow[i]
        high = (seg >> 9) * 4 + ((seg >> 3) & 3)
        value = jnp.where(sub16 == high, faces[i], 0.0)
        left = thirds(value)
        total = total + lax.dot_general(
            left, hot[i], (((1,), (1,)), ((), ())), preferred_element_type=F32
        )
    sums = total[0:16] + total[16:32] + total[32:48]
    for h in range(16):
        part[h] = sums[h : h + 1, :]

    copies = []
    for h in plane_order:
        dev = plane(h)
        row = (dev[0] // 16) * 4 + dev[1]
        cp = pltpu.make_async_remote_copy(
            part.at[row], got1.at[h], r_send.at[0, h], r_recv.at[0, h], device_id=dev, device_id_type=MESH
        )
        cp.start()
        copies.append(cp)
    for cp in near:
        cp.wait_recv()
    for rim in rims:
        setup_low(1 + DEPTH, pl.ds(rim[2], rim[3] - rim[2]))
        for i in range(1, 7):
            setup(i + DEPTH, rim)
        run(1, range(1, 7), rim)
    send_x(2)
    for rim in rims2:
        run(2, range(2, 6), rim)
    send_x(3)
    run(3, (3, 4))

    for cp in first:
        cp.wait_recv()
    setup_low(DEPTH)
    for i in (0, 7):
        setup(i + DEPTH)
    run(1, (0, 7))
    run(2, (1, 6))
    run(3, (2, 5))
    send_x(4)
    for cp in first2:
        cp.wait_recv()
    setup_low(-1 + DEPTH)
    for i in (-1, 8):
        setup(i + DEPTH)
    run(1, (-1, 8))
    run(2, (0, 7))
    run(3, (1, 6))
    run(4, (2, 5))
    send_x(5)
    run(4, (3, 4))
    run(5, (3, 4))

    for cp in second:
        cp.wait_recv()
    setup_low(-2 + DEPTH)
    for i in (-2, 9):
        setup(i + DEPTH)
    run(1, (-2, 9))
    run(2, (-1, 8))
    run(3, (0, 7))
    run(4, (1, 6))
    run(5, (2, 5))
    run(6, (3, 4))

    acc = part[my_y * 4 + gy]
    for h, cp in zip(plane_order, copies):
        cp.wait_recv()
        acc = acc + got1[h]
    row2[...] = acc
    more = []
    for h in column_order:
        cp = pltpu.make_async_remote_copy(
            row2, got2.at[h], r_send.at[1, h], r_recv.at[1, h], device_id=column(h), device_id_type=MESH
        )
        cp.start()
        more.append(cp)

    for n in (2, 3):
        for side in (0, 1):
            x_copies[side, n].wait_recv()
    run(2, (-2, 9))
    run(3, (-2, -1, 8, 9))
    run(4, (-1, 0, 7, 8))
    run(5, (0, 1, 6, 7))
    run(6, (1, 2, 5, 6))
    run(7, (2, 3, 4, 5))

    for side in (0, 1):
        x_copies[side, 4].wait_recv()
    run(4, (-2, 9))
    run(5, (-1, 8))
    run(6, (0, 7))
    run(7, (1, 6))

    for side in (0, 1):
        x_copies[side, 5].wait_recv()
    run(5, (-2, 9))
    run(6, (-1, 8))
    run(7, (0, 7))

    acc = row2[...]
    for h, cp in zip(column_order, more):
        cp.wait_recv()
        acc = acc + got2[h]
    owned = (my_z * 2 + my_c) * 8
    grad[...] = -pltpu.roll(jnp.broadcast_to(acc, (8, LANES)), lax.rem(LANES - owned, LANES), 1)

    for cp in sends + list(x_copies.values()) + copies + more:
        cp.wait_send()


def body(cot, cap, cond, gap, tc, ids):
    wide = pltpu.VMEM((TALL, WIDE, LANES), F32)
    n_static = 8 + 4 + 8 + 8 + 2 + 2 + 4 + 4 + 2
    adjoint, grad = pl.pallas_call(
        kernel,
        out_shape=(
            jax.ShapeDtypeStruct((ROWS, COLS, LANES), F32),
            jax.ShapeDtypeStruct((8, LANES), F32),
        ),
        in_specs=[pl.BlockSpec(memory_space=pltpu.HBM)] * 6,
        out_specs=(pl.BlockSpec(memory_space=pltpu.VMEM), pl.BlockSpec(memory_space=pltpu.VMEM)),
        scratch_shapes=[wide] * 9
        + [
            pltpu.VMEM((ITERS - 2, TALL, WIDE, LANES), F32),
            pltpu.VMEM((ROWS, COLS), F32),
            pltpu.SMEM((2048,), F32),
            pltpu.SMEM((ROWS, 16), jnp.int32),
            pltpu.VMEM((ROWS, LANES, LANES), jnp.bfloat16),
            pltpu.VMEM((ROWS, 1, LANES), jnp.int32),
            pltpu.VMEM((ROWS, 8, LANES), F32),
            pltpu.VMEM((16, 1, LANES), F32),
            pltpu.VMEM((16, 1, LANES), F32),
            pltpu.VMEM((1, LANES), F32),
            pltpu.VMEM((16, 1, LANES), F32),
            pltpu.VMEM((ROWS, 4, 8, LANES), F32),
            pltpu.VMEM((SLAB, 4, 8, LANES), F32),
            pltpu.VMEM((2, 3 * REACH + 1, 8, LANES), F32),
            pltpu.VMEM((2, 3 * REACH + 1, 8, LANES), F32),
            pltpu.VMEM((2, 2, 8, LANES), F32),
            pltpu.VMEM((2, 3, 2, 8, LANES), F32),
            pltpu.VMEM((13, SLAB, 8, LANES), F32),
            pltpu.SemaphoreType.DMA((6,)),
            pltpu.SemaphoreType.DMA((n_static,)),
            pltpu.SemaphoreType.DMA((n_static,)),
            pltpu.SemaphoreType.DMA((2, 4)),
            pltpu.SemaphoreType.DMA((2, 4)),
            pltpu.SemaphoreType.DMA((2, 16)),
            pltpu.SemaphoreType.DMA((2, 16)),
        ],
        compiler_params=pltpu.CompilerParams(
            collective_id=0, has_side_effects=True, vmem_limit_bytes=48 * 1024 * 1024
        ),
    )(*(pltpu.with_memory_space_constraint(v, pltpu.HBM) for v in (cot, cap, cond, gap, tc, ids)))
    return adjoint, grad[0, 0:8]


def solution(mesh):
    in_specs = (
        P("gx", "gy", None),
        P("gx", "gy", None),
        P("gx", "gy", None),
        P("gx", "gy"),
        P(),
        P("gx", "gy"),
    )
    out_specs = (P("gx", "gy", None), P(("gx", "gy")))
    return jax.shard_map(body, mesh=mesh, in_specs=in_specs, out_specs=out_specs, check_vma=False)
```

```python
import functools

import jax
import jax.numpy as jnp
from jax import lax
from jax.experimental import pallas as pl
from jax.experimental.pallas import tpu as pltpu
from jax.sharding import PartitionSpec as P

MESH = pl.DeviceIdType.MESH
F32 = jnp.float32
ITERS = 8
LOW_BOUND = 0.2
HIGH_BOUND = 28.0
THETA = (HIGH_BOUND + LOW_BOUND) / 2.0
DELTA = (HIGH_BOUND - LOW_BOUND) / 2.0
SIGMA = THETA / DELTA

ROWS, COLS, LANES = 8, 128, 128
DEPTH = 3
SIDE = 8
WIDE = COLS + 2 * SIDE
TALL = ROWS + 2 * DEPTH
REACH = ITERS - 1
SLAB = ROWS + 2 * REACH
OWN_ROWS = pl.ds(DEPTH, ROWS)
OWN_COLS = pl.ds(SIDE, COLS)


def coefficients():
    ratio = 1.0 / SIGMA
    out = []
    for _ in range(ITERS - 1):
        new = 1.0 / (2.0 * SIGMA - ratio)
        out.append((new * ratio, 2.0 * new / DELTA))
        ratio = new
    return out


COEF = coefficients()


def kernel(
    cot, cap, cond, gap_in, tc_in, ids_in,
    out, grad,
    B, C, G, DG, WX, WYp, WYm, WZp, WZm, X, gap, tc, ids, hot, idrow, spread, part, got1, row2, got2,
    SP, SF, SB, RB, ES, ER, SX,
    loc_sem, st_send, st_recv, x_send, x_recv, r_send, r_recv,
):
    gx, gy = lax.axis_index("gx"), lax.axis_index("gy")
    nx, ny = 64, 4
    my_y, my_z, my_c = gx // 16, lax.rem(gx // 2, 8), lax.rem(gx, 2)

    def at(dx, dy):
        return (lax.rem(gx + dx + nx, nx), lax.rem(gy + dy + ny, ny))

    def plane(h):
        return (lax.rem(my_y + h // 4, 4) * 16 + my_z * 2 + my_c, lax.rem(gy + h % 4, 4))

    def column(h):
        return (my_y * 16 + lax.rem(my_z + h // 2, 8) * 2 + lax.rem(my_c + h % 2, 2), gy)

    plane_order = sorted(range(1, 16), key=lambda h: -min(h // 4, 4 - h // 4) - min(h % 4, 4 - h % 4))
    column_order = sorted(range(1, 16), key=lambda h: -min(h // 2, 8 - h // 2) - (h % 2) / 2)

    barrier = pltpu.get_barrier_semaphore()
    around = [(dx, dy) for dx in (-1, 0, 1) for dy in (-1, 0, 1) if dx or dy]
    partners = [at(*d) for d in around] + [plane(h) for h in range(1, 16)] + [column(h) for h in range(1, 16)]
    for dev in partners:
        pl.semaphore_signal(barrier, inc=1, device_id=dev, device_id_type=MESH)

    loads = [
        pltpu.make_async_copy(cot, B.at[OWN_ROWS, OWN_COLS], loc_sem.at[0]),
        pltpu.make_async_copy(cond, C.at[OWN_ROWS, OWN_COLS], loc_sem.at[1]),
        pltpu.make_async_copy(cap, G.at[OWN_ROWS, OWN_COLS], loc_sem.at[2]),
        pltpu.make_async_copy(gap_in, gap, loc_sem.at[3]),
        pltpu.make_async_copy(tc_in, tc, loc_sem.at[4]),
        pltpu.make_async_copy(ids_in, ids, loc_sem.at[5]),
    ]
    for cp in loads:
        cp.start()

    sends = []
    counter = [0]

    def push(src, dst, dev):
        k = counter[0]
        counter[0] += 1
        cp = pltpu.make_async_remote_copy(
            src, dst, st_send.at[k], st_recv.at[k], device_id=dev, device_id_type=MESH
        )
        cp.start()
        sends.append(cp)
        return cp

    def rows_for(dx, depth_from, count):
        if dx > 0:
            first = ROWS - (depth_from + count - 1)
            return pl.ds(first, count), pl.ds(DEPTH - (depth_from + count - 1), count)
        return pl.ds(depth_from - 1, count), pl.ds(DEPTH + ROWS + depth_from - 1, count)

    def cols_for(dy):
        if dy > 0:
            return pl.ds(COLS - SIDE, SIDE), pl.ds(0, SIDE)
        if dy < 0:
            return pl.ds(0, SIDE), pl.ds(SIDE + COLS, SIDE)
        return pl.ds(0, COLS), OWN_COLS

    for k in (0, 1, 2, 4, 5):
        loads[k].wait()
    lane8 = lax.broadcasted_iota(jnp.int32, (8, LANES), 1)
    lane1 = lax.broadcasted_iota(jnp.int32, (1, LANES), 1)

    def face_row(i, _):
        vec = jnp.zeros((1, LANES), jnp.int32)
        for jb in range(16):
            seg = ids[i, jb]
            value = tc[seg]
            cols = pl.ds(SIDE + 8 * jb, 8)
            G[DEPTH + i, cols, :] = G[DEPTH + i, cols, :] + jnp.where(lane8 == 0, value, 0.0)
            vec = jnp.where(lane1 == REACH * (jb + 1), seg, vec)
        idrow[i, :, :] = vec
        return 0

    lax.fori_loop(0, ROWS, face_row, 0)

    sub8 = lax.broadcasted_iota(jnp.int32, (8, LANES), 0)
    height = lax.rem(lane8, REACH)
    low, top = height == 0, height == REACH - 1

    def pack_row(i, _):
        b = c = g = b7 = c7 = jnp.zeros((8, LANES), F32)
        for jb in range(16):
            cols = pl.ds(SIDE + 8 * jb, 8)
            at0 = REACH * (jb + 1)
            here = jnp.logical_and(lane8 >= at0, lane8 < at0 + REACH)
            over = lane8 == at0 + REACH
            vb = pltpu.roll(B[DEPTH + i, cols, :], at0, 1)
            vc = pltpu.roll(C[DEPTH + i, cols, :], at0, 1)
            vg = pltpu.roll(G[DEPTH + i, cols, :], at0, 1)
            b, c, g = jnp.where(here, vb, b), jnp.where(here, vc, c), jnp.where(here, vg, g)
            b7, c7 = jnp.where(over, vb, b7), jnp.where(over, vc, c7)
        b7, c7 = pltpu.roll(b7, LANES - 1, 1), pltpu.roll(c7, LANES - 1, 1)
        above = jnp.where(top, c7, pltpu.roll(c, LANES - 1, 1))
        below = jnp.where(low, 0.0, pltpu.roll(c, 1, 1))
        SP[i, 0] = b
        SP[i, 1] = c
        SP[i, 2] = g + c + 0.5 * (above + below)
        SP[i, 3] = jnp.where(top, 0.5 * (c + c7) * b7, 0.0)
        return 0

    lax.fori_loop(0, ROWS, pack_row, 0)
    for side, row0 in ((0, 1), (1, 0)):
        terms = jnp.zeros((8, LANES), F32)
        for k in range(REACH):
            for arr in range(3):
                SB[side, 3 * k + arr] = SP[row0 + k, arr]
            terms = jnp.where(height == k, pltpu.roll(SP[row0 + k, 3], (k - REACH + 1) % LANES, 1), terms)
        SB[side, 3 * REACH] = terms
    HALF = REACH * ROWS
    for side, block in ((0, 16), (1, 1)):
        tiles = [jnp.zeros((8, LANES), F32)] * 2
        for r in range(ROWS):
            for arr, tile, to, width in ((0, 0, REACH * r, REACH), (1, 0, HALF + REACH * r, REACH),
                                         (2, 1, REACH * r, REACH), (3, 1, HALF + r, 1)):
                start = REACH * block + (REACH - 1 if arr == 3 else 0)
                moved = pltpu.roll(SP[r, arr], (to - start) % LANES, 1)
                tiles[tile] = jnp.where(jnp.logical_and(lane8 >= to, lane8 < to + width), moved, tiles[tile])
        ES[side, 0], ES[side, 1] = tiles

    pl.semaphore_wait(barrier, len(partners))

    layer = []
    for dx in (1, -1):
        for side, dy in ((0, 1), (1, -1)):
            layer.append(push(ES.at[side], ER.at[side, dx + 1], at(dx, dy)))
    for side, dx in ((0, 1), (1, -1)):
        layer.append(push(SB.at[side], RB.at[side], at(dx, 0)))
    for side, dy in ((0, 1), (1, -1)):
        layer.append(push(ES.at[side], ER.at[side, 1], at(0, dy)))

    near, first, second = [], [], []
    pairs = ((cot, B), (cond, C))
    for src, dst in pairs:
        for dy in (1, -1):
            sc, dc = cols_for(dy)
            near.append(push(src.at[:, sc], dst.at[OWN_ROWS, dc], at(0, dy)))
    first2 = []
    for depth, group in ((1, first), (2, first2)):
        for src, dst in pairs:
            for dx in (1, -1):
                sr, dr = rows_for(dx, depth, 1)
                group.append(push(src.at[sr], dst.at[dr, OWN_COLS], at(dx, 0)))
    for src, dst in pairs:
        for dx in (1, -1):
            for dy in (1, -1):
                sr, dr = rows_for(dx, 1, 3)
                sc, dc = cols_for(dy)
                first.append(push(src.at[sr, sc], dst.at[dr, dc], at(dx, dy)))

    for dy in (1, -1):
        sc, dc = cols_for(dy)
        src_cols = pl.ds(SIDE + sc.start, sc.size)
        near.append(push(G.at[OWN_ROWS, src_cols], G.at[OWN_ROWS, dc], at(0, dy)))
    for dx in (1, -1):
        sr, dr = rows_for(dx, 1, 1)
        first2.append(push(G.at[pl.ds(DEPTH + sr.start, 1), OWN_COLS], G.at[dr, OWN_COLS], at(dx, 0)))
    for dx in (1, -1):
        for dy in (1, -1):
            sr, dr = rows_for(dx, 1, 2)
            sc, dc = cols_for(dy)
            first2.append(
                push(
                    G.at[pl.ds(DEPTH + sr.start, 2), pl.ds(SIDE + sc.start, SIDE)],
                    G.at[dr, dc],
                    at(dx, dy),
                )
            )
    for src, dst in pairs:
        for dx in (1, -1):
            sr, dr = rows_for(dx, 3, 1)
            second.append(push(src.at[sr], dst.at[dr, OWN_COLS], at(dx, 0)))
    for dx in (1, -1):
        sr, dr = rows_for(dx, 2, 1)
        second.append(push(G.at[pl.ds(DEPTH + sr.start, 1), OWN_COLS], G.at[dr, OWN_COLS], at(dx, 0)))

    inner = (SIDE, SIDE + COLS, SIDE + 8, SIDE + COLS - 8)
    inner2 = (SIDE + 8, SIDE + COLS - 8, SIDE + 16, SIDE + COLS - 16)
    rims = ((0, SIDE + 16, 0, SIDE + 8), (SIDE + COLS - 16, WIDE, SIDE + COLS - 8, WIDE))
    rims2 = ((0, SIDE + 24, 0, SIDE + 16), (SIDE + COLS - 24, WIDE, SIDE + COLS - 16, WIDE))

    def window(span):
        lo, hi, start, stop = span
        return pl.ds(lo, hi - lo), hi - lo, pl.ds(start, stop - start), lambda v: v[start - lo : stop - lo]

    def setup(r, span=(0, WIDE, 0, WIDE)):
        read, width, keep, cut = window(span)
        col = lax.broadcasted_iota(jnp.int32, (span[3] - span[2], LANES), 0) + span[2]
        lane = lax.broadcasted_iota(jnp.int32, (span[3] - span[2], LANES), 1)
        left_edge = jnp.logical_and(col == SIDE, gy == 0)
        right_edge = jnp.logical_and(col == SIDE + COLS - 1, gy == ny - 1)
        line = C[r, read, :]
        centre = cut(line)
        up = jnp.where(jnp.logical_and(r == DEPTH + ROWS - 1, gx == nx - 1), 0.0, C[r + 1, keep, :])
        down = jnp.where(jnp.logical_and(r == DEPTH, gx == 0), 0.0, C[r - 1, keep, :])
        right = jnp.where(right_edge, 0.0, cut(pltpu.roll(line, width - 1, 0)))
        left = jnp.where(left_edge, 0.0, cut(pltpu.roll(line, 1, 0)))
        above = jnp.where(lane == LANES - 1, 0.0, pltpu.roll(centre, LANES - 1, 1))
        below = jnp.where(lane == 0, 0.0, pltpu.roll(centre, 1, 1))
        DG[r, keep, :] = G[r, keep, :] + (
            3.0 * centre + 0.5 * ((up + down) + (right + left) + (above + below))
        )
        WYp[r, keep, :] = jnp.where(right_edge, 0.0, 0.5 * (centre + right))
        WYm[r, keep, :] = jnp.where(left_edge, 0.0, 0.5 * (centre + left))
        WZp[r, keep, :] = jnp.where(lane == LANES - 1, 0.0, 0.5 * (centre + above))
        WZm[r, keep, :] = jnp.where(lane == 0, 0.0, 0.5 * (centre + below))
        outer = jnp.logical_or(
            jnp.logical_and(r == DEPTH + ROWS - 1, gx == nx - 1), jnp.logical_and(r == DEPTH - 1, gx == 0)
        )
        WX[r, keep, :] = jnp.where(outer, 0.0, 0.5 * (centre + up))

    def setup_low(r, keep=pl.ds(0, WIDE)):
        WX[r - 1, keep, :] = jnp.where(
            jnp.logical_and(r == DEPTH, gx == 0), 0.0, 0.5 * (C[r, keep, :] + C[r - 1, keep, :])
        )

    def step(n, r, span):
        a, beta = COEF[n - 1]
        read, width, keep, cut = window(span)
        src = B if n == 1 else X.at[n - 2]
        line = src[r, read, :]
        x = cut(line)
        acc = WX[r, keep, :] * src[r + 1, keep, :] + WX[r - 1, keep, :] * src[r - 1, keep, :]
        acc += WYp[r, keep, :] * cut(pltpu.roll(line, width - 1, 0)) + WYm[r, keep, :] * cut(pltpu.roll(line, 1, 0))
        acc += WZp[r, keep, :] * pltpu.roll(x, LANES - 1, 1) + WZm[r, keep, :] * pltpu.roll(x, 1, 1)
        acc = acc - DG[r, keep, :] * x
        if n == 1:
            return ((1.0 + a) / THETA + beta) * x + (beta / THETA) * acc
        b = B[r, keep, :]
        if n == 2:
            return (1.0 + a) * x + (beta - a / THETA) * b + beta * acc
        return (1.0 + a) * x - a * X[n - 3, r, keep, :] + beta * (b + acc)

    def run(n, rows, span=(0, WIDE, 0, WIDE)):
        for i in rows:
            new = step(n, i + DEPTH, span)
            if n < ITERS - 1:
                X[n - 1, i + DEPTH, pl.ds(span[2], span[3] - span[2]), :] = new
            else:
                out[i] = new[SIDE : SIDE + COLS]

    x_copies = {}

    def send_x(n):
        for side, dx, src_row, dst_row in ((0, 1, 5, 0), (1, -1, 2, TALL - 1)):
            cp = pltpu.make_async_remote_copy(
                X.at[n - 2, DEPTH + src_row], X.at[n - 2, dst_row],
                x_send.at[side, n - 2], x_recv.at[side, n - 2],
                device_id=at(dx, 0), device_id_type=MESH,
            )
            cp.start()
            x_copies[side, n] = cp

    loads[3].wait()
    pick = [jnp.where(lax.rem(lane8, 8) == sub8, gap[i : i + 1, :], 0.0) for i in range(ROWS)]
    target = (lax.broadcasted_iota(jnp.int32, (LANES, LANES), 0) // 8 + 1) * REACH
    place = jnp.where(lax.broadcasted_iota(jnp.int32, (LANES, LANES), 1) == target, 1.0, 0.0).astype(jnp.bfloat16)

    def thirds(value):
        v1 = value.astype(jnp.bfloat16).astype(F32)
        v2 = (value - v1).astype(jnp.bfloat16).astype(F32)
        return jnp.concatenate([v1, v2, value - v1 - v2], axis=0).astype(jnp.bfloat16)

    laid = jnp.dot(thirds(jnp.concatenate(pick, axis=0)), place, preferred_element_type=F32)
    laid = laid[0:64] + laid[64:128] + laid[128:192]
    for i in range(ROWS):
        spread[i] = laid[8 * i : 8 * i + 8, :]

    sub128 = lax.broadcasted_iota(jnp.int32, (LANES, LANES), 0)

    def one_hot(i, _):
        seg = idrow[i]
        low = ((seg >> 5) & 15) * 8 + (seg & 7)
        hot[i] = jnp.where(sub128 == low, 1.0, 0.0).astype(jnp.bfloat16)
        return 0

    lax.fori_loop(0, ROWS, one_hot, 0)

    setup_low(1 + DEPTH, pl.ds(inner[2], inner[3] - inner[2]))
    for i in range(1, 7):
        setup(i + DEPTH, inner)
    run(1, range(1, 7), inner)
    run(2, range(2, 6), inner2)

    for cp in layer:
        cp.wait_recv()
    head = lane8 < REACH
    tail = jnp.logical_and(lane8 >= 17 * REACH, lane8 < 18 * REACH)
    for dx in (-1, 0, 1):
        for r in range(ROWS):
            q = REACH + r - ROWS * dx
            if not 0 <= q < SLAB:
                continue
            for arr, tile, start in ((0, 0, REACH * r), (1, 0, HALF + REACH * r), (2, 1, REACH * r), (3, 1, HALF + r)):
                skip = REACH - 1 if arr == 3 else 0
                if dx == 0:
                    own = SP[r, arr]
                elif arr < 3:
                    own = RB[0 if dx > 0 else 1, 3 * (r - (1 if dx > 0 else 0)) + arr]
                else:
                    k = r - (1 if dx > 0 else 0)
                    own = pltpu.roll(RB[0 if dx > 0 else 1, 3 * REACH], REACH - 1 - k, 1)
                left = pltpu.roll(ER[0, dx + 1, tile], (skip - start) % LANES, 1)
                right = pltpu.roll(ER[1, dx + 1, tile], (17 * REACH + skip - start) % LANES, 1)
                row = jnp.where(head, left, jnp.where(tail, right, own))
                SF[q, arr] = jnp.where(top, row, 0.0) if arr == 3 else row

    def next_col(v):
        t = pltpu.roll(v, 7, 1)
        return jnp.where(lax.broadcasted_iota(jnp.int32, v.shape, 1) == 7, pltpu.roll(t, LANES - REACH, 2), t)

    def last_col(v):
        t = pltpu.roll(v, 1, 1)
        return jnp.where(lax.broadcasted_iota(jnp.int32, v.shape, 1) == 0, pltpu.roll(t, REACH, 2), t)

    def in_block(shape, block):
        spot = lax.broadcasted_iota(jnp.int32, shape, 2)
        return jnp.logical_and(spot >= REACH * block, spot < REACH * (block + 1))

    mid = (SLAB - 2, 8, LANES)
    rows_ = lax.broadcasted_iota(jnp.int32, mid, 0) + 1
    subs_ = lax.broadcasted_iota(jnp.int32, mid, 1)
    high_ = lax.rem(lax.broadcasted_iota(jnp.int32, mid, 2), REACH)
    off_up = jnp.logical_and(rows_ == REACH + ROWS - 1, gx == nx - 1)
    off_down = jnp.logical_and(rows_ == REACH, gx == 0)
    off_right = jnp.logical_and(jnp.logical_and(in_block(mid, 16), subs_ == 7), gy == ny - 1)
    off_left = jnp.logical_and(jnp.logical_and(in_block(mid, 1), subs_ == 0), gy == 0)
    sc_ = SF[1 : SLAB - 1, 1]
    near_cond = [
        jnp.where(off_up, 0.0, SF[2:SLAB, 1]),
        jnp.where(off_down, 0.0, SF[0 : SLAB - 2, 1]),
        jnp.where(off_right, 0.0, next_col(sc_)),
        jnp.where(off_left, 0.0, last_col(sc_)),
    ]
    diag_ = SF[1 : SLAB - 1, 2] + 2.0 * sc_
    weight = []
    for off, other in zip((off_up, off_down, off_right, off_left), near_cond):
        diag_ = diag_ + 0.5 * other
        weight.append(jnp.where(off, 0.0, 0.5 * (sc_ + other)))
    weight.append(jnp.where(high_ == REACH - 1, 0.0, 0.5 * (sc_ + pltpu.roll(sc_, LANES - 1, 2))))
    weight.append(jnp.where(high_ == 0, 0.0, 0.5 * (sc_ + pltpu.roll(sc_, 1, 2))))
    for k, w in enumerate(weight):
        SX[k, 1 : SLAB - 1] = w
    SX[6, 1 : SLAB - 1] = diag_

    for n in range(1, ITERS):
        a, beta = COEF[n - 1]
        lo, hi = n, SLAB - n

        def state(m, p, q):
            return SF[p:q, 0] if m == 1 else SX[5 + m, p:q]

        x = state(n, lo, hi)
        acc = SX[0, lo:hi] * state(n, lo + 1, hi + 1) + SX[1, lo:hi] * state(n, lo - 1, hi - 1)
        acc += SX[2, lo:hi] * next_col(x) + SX[3, lo:hi] * last_col(x)
        acc += SX[4, lo:hi] * pltpu.roll(x, LANES - 1, 2) + SX[5, lo:hi] * pltpu.roll(x, 1, 2)
        acc = acc - SX[6, lo:hi] * x
        b = SF[lo:hi, 0]
        if n == 1:
            new = ((1.0 + a) / THETA + beta) * x + (beta / THETA) * (acc + SF[lo:hi, 3])
        elif n == 2:
            new = (1.0 + a) * x + (beta - a / THETA) * b + beta * acc
        else:
            new = (1.0 + a) * x - a * state(n - 1, lo, hi) + beta * (b + acc)
        if n < ITERS - 1:
            SX[6 + n, lo:hi] = new
    faces = jnp.sum(new * spread[...], axis=1, keepdims=True)

    sub16 = lax.broadcasted_iota(jnp.int32, (16, LANES), 0)
    total = jnp.zeros((48, LANES), F32)
    for i in range(ROWS):
        seg = idrow[i]
        high = (seg >> 9) * 4 + ((seg >> 3) & 3)
        value = jnp.where(sub16 == high, faces[i], 0.0)
        left = thirds(value)
        total = total + lax.dot_general(
            left, hot[i], (((1,), (1,)), ((), ())), preferred_element_type=F32
        )
    sums = total[0:16] + total[16:32] + total[32:48]
    for h in range(16):
        part[h] = sums[h : h + 1, :]

    def all_in(box, sem):
        pltpu.make_async_copy(box.at[pl.ds(1, 15)], box.at[pl.ds(1, 15)], sem).wait()

    for h in plane_order:
        dev = plane(h)
        row = (dev[0] // 16) * 4 + dev[1]
        cp = pltpu.make_async_remote_copy(
            part.at[row], got1.at[h], r_send.at[0], r_recv.at[0], device_id=dev, device_id_type=MESH
        )
        cp.start()
    for cp in near:
        cp.wait_recv()
    for rim in rims:
        setup_low(1 + DEPTH, pl.ds(rim[2], rim[3] - rim[2]))
        for i in range(1, 7):
            setup(i + DEPTH, rim)
        run(1, range(1, 7), rim)
    send_x(2)
    for rim in rims2:
        run(2, range(2, 6), rim)
    send_x(3)
    run(3, (3, 4))

    for cp in first:
        cp.wait_recv()
    setup_low(DEPTH)
    for i in (0, 7):
        setup(i + DEPTH)
    run(1, (0, 7))
    run(2, (1, 6))
    run(3, (2, 5))
    send_x(4)
    for cp in first2:
        cp.wait_recv()
    setup_low(-1 + DEPTH)
    for i in (-1, 8):
        setup(i + DEPTH)
    run(1, (-1, 8))
    run(2, (0, 7))
    run(3, (1, 6))
    run(4, (2, 5))
    send_x(5)
    run(4, (3, 4))
    run(5, (3, 4))

    for cp in second:
        cp.wait_recv()
    setup_low(-2 + DEPTH)
    for i in (-2, 9):
        setup(i + DEPTH)
    run(1, (-2, 9))
    run(2, (-1, 8))
    run(3, (0, 7))
    run(4, (1, 6))
    run(5, (2, 5))
    run(6, (3, 4))

    all_in(got1, r_recv.at[0])
    acc = part[my_y * 4 + gy] + jnp.sum(got1[1:16], axis=0)
    row2[...] = acc
    for h in column_order:
        cp = pltpu.make_async_remote_copy(
            row2, got2.at[h], r_send.at[1], r_recv.at[1], device_id=column(h), device_id_type=MESH
        )
        cp.start()

    for n in (2, 3):
        for side in (0, 1):
            x_copies[side, n].wait_recv()
    run(2, (-2, 9))
    run(3, (-2, -1, 8, 9))
    run(4, (-1, 0, 7, 8))
    run(5, (0, 1, 6, 7))
    run(6, (1, 2, 5, 6))
    run(7, (2, 3, 4, 5))

    for cp in sends:
        cp.wait_send()
    all_in(got1, r_send.at[0])
    for side in (0, 1):
        x_copies[side, 4].wait_recv()
    run(4, (-2, 9))
    run(5, (-1, 8))
    run(6, (0, 7))
    run(7, (1, 6))

    for cp in x_copies.values():
        cp.wait_send()
    for side in (0, 1):
        x_copies[side, 5].wait_recv()
    run(5, (-2, 9))
    run(6, (-1, 8))
    run(7, (0, 7))

    all_in(got2, r_recv.at[1])
    acc = row2[...] + jnp.sum(got2[1:16], axis=0)
    owned = (my_z * 2 + my_c) * 8
    grad[...] = -pltpu.roll(jnp.broadcast_to(acc, (8, LANES)), lax.rem(LANES - owned, LANES), 1)

    all_in(got2, r_send.at[1])


def body(cot, cap, cond, gap, tc, ids):
    wide = pltpu.VMEM((TALL, WIDE, LANES), F32)
    n_static = 8 + 4 + 8 + 8 + 2 + 2 + 4 + 4 + 2
    adjoint, grad = pl.pallas_call(
        kernel,
        out_shape=(
            jax.ShapeDtypeStruct((ROWS, COLS, LANES), F32),
            jax.ShapeDtypeStruct((8, LANES), F32),
        ),
        in_specs=[pl.BlockSpec(memory_space=pltpu.HBM)] * 6,
        out_specs=(pl.BlockSpec(memory_space=pltpu.VMEM), pl.BlockSpec(memory_space=pltpu.VMEM)),
        scratch_shapes=[wide] * 9
        + [
            pltpu.VMEM((ITERS - 2, TALL, WIDE, LANES), F32),
            pltpu.VMEM((ROWS, COLS), F32),
            pltpu.SMEM((2048,), F32),
            pltpu.SMEM((ROWS, 16), jnp.int32),
            pltpu.VMEM((ROWS, LANES, LANES), jnp.bfloat16),
            pltpu.VMEM((ROWS, 1, LANES), jnp.int32),
            pltpu.VMEM((ROWS, 8, LANES), F32),
            pltpu.VMEM((16, 1, LANES), F32),
            pltpu.VMEM((16, 1, LANES), F32),
            pltpu.VMEM((1, LANES), F32),
            pltpu.VMEM((16, 1, LANES), F32),
            pltpu.VMEM((ROWS, 4, 8, LANES), F32),
            pltpu.VMEM((SLAB, 4, 8, LANES), F32),
            pltpu.VMEM((2, 3 * REACH + 1, 8, LANES), F32),
            pltpu.VMEM((2, 3 * REACH + 1, 8, LANES), F32),
            pltpu.VMEM((2, 2, 8, LANES), F32),
            pltpu.VMEM((2, 3, 2, 8, LANES), F32),
            pltpu.VMEM((13, SLAB, 8, LANES), F32),
            pltpu.SemaphoreType.DMA((6,)),
            pltpu.SemaphoreType.DMA((n_static,)),
            pltpu.SemaphoreType.DMA((n_static,)),
            pltpu.SemaphoreType.DMA((2, 4)),
            pltpu.SemaphoreType.DMA((2, 4)),
            pltpu.SemaphoreType.DMA((2,)),
            pltpu.SemaphoreType.DMA((2,)),
        ],
        compiler_params=pltpu.CompilerParams(
            collective_id=0, has_side_effects=True, vmem_limit_bytes=48 * 1024 * 1024
        ),
    )(*(pltpu.with_memory_space_constraint(v, pltpu.HBM) for v in (cot, cap, cond, gap, tc, ids)))
    return adjoint, grad[0, 0:8]


def solution(mesh):
    in_specs = (
        P("gx", "gy", None),
        P("gx", "gy", None),
        P("gx", "gy", None),
        P("gx", "gy"),
        P(),
        P("gx", "gy"),
    )
    out_specs = (P("gx", "gy", None), P(("gx", "gy")))
    return jax.shard_map(body, mesh=mesh, in_specs=in_specs, out_specs=out_specs, check_vma=False)
```

```python
import functools

import jax
import jax.numpy as jnp
from jax import lax
from jax.experimental import pallas as pl
from jax.experimental.pallas import tpu as pltpu
from jax.sharding import PartitionSpec as P

MESH = pl.DeviceIdType.MESH
F32 = jnp.float32
ITERS = 8
LOW_BOUND = 0.2
HIGH_BOUND = 28.0
THETA = (HIGH_BOUND + LOW_BOUND) / 2.0
DELTA = (HIGH_BOUND - LOW_BOUND) / 2.0
SIGMA = THETA / DELTA

ROWS, COLS, LANES = 8, 128, 128
DEPTH = 3
SIDE = 8
WIDE = COLS + 2 * SIDE
TALL = ROWS + 2 * DEPTH
REACH = ITERS - 1
SLAB = ROWS + 2 * REACH
OWN_ROWS = pl.ds(DEPTH, ROWS)
OWN_COLS = pl.ds(SIDE, COLS)


def coefficients():
    ratio = 1.0 / SIGMA
    out = []
    for _ in range(ITERS - 1):
        new = 1.0 / (2.0 * SIGMA - ratio)
        out.append((new * ratio, 2.0 * new / DELTA))
        ratio = new
    return out


COEF = coefficients()


def kernel(
    cot, cap, cond, gap_in, tc_in, ids_in,
    out, grad,
    B, C, G, DG, WX, WYp, WYm, WZp, WZm, X, gap, tc, ids, hot, idrow, spread, part, got1, row2, got2,
    SP, SF, SB, RB, ES, ER, SX,
    loc_sem, st_send, st_recv, x_send, x_recv, r_send, r_recv,
):
    gx, gy = lax.axis_index("gx"), lax.axis_index("gy")
    nx, ny = 64, 4
    my_y, my_z, my_c = gx // 16, lax.rem(gx // 2, 8), lax.rem(gx, 2)

    def at(dx, dy):
        return (lax.rem(gx + dx + nx, nx), lax.rem(gy + dy + ny, ny))

    def plane(h):
        return (lax.rem(my_y + h // 4, 4) * 16 + my_z * 2 + my_c, lax.rem(gy + h % 4, 4))

    def column(h):
        return (my_y * 16 + lax.rem(my_z + h // 2, 8) * 2 + lax.rem(my_c + h % 2, 2), gy)

    plane_order = sorted(range(1, 16), key=lambda h: -min(h // 4, 4 - h // 4) - min(h % 4, 4 - h % 4))
    column_order = sorted(range(1, 16), key=lambda h: -min(h // 2, 8 - h // 2) - (h % 2) / 2)

    barrier = pltpu.get_barrier_semaphore()
    around = [(dx, dy) for dx in (-1, 0, 1) for dy in (-1, 0, 1) if dx or dy]
    partners = [at(*d) for d in sorted(around, key=lambda d: -abs(d[0]) - abs(d[1]))] + [column(h) for h in column_order] + [plane(h) for h in plane_order]
    for dev in partners:
        pl.semaphore_signal(barrier, inc=1, device_id=dev, device_id_type=MESH)

    loads = [
        pltpu.make_async_copy(cot, B.at[OWN_ROWS, OWN_COLS], loc_sem.at[0]),
        pltpu.make_async_copy(cond, C.at[OWN_ROWS, OWN_COLS], loc_sem.at[1]),
        pltpu.make_async_copy(cap, G.at[OWN_ROWS, OWN_COLS], loc_sem.at[2]),
        pltpu.make_async_copy(gap_in, gap, loc_sem.at[3]),
        pltpu.make_async_copy(tc_in, tc, loc_sem.at[4]),
        pltpu.make_async_copy(ids_in, ids, loc_sem.at[5]),
    ]
    for cp in loads:
        cp.start()

    sends = []
    counter = [0]

    def push(src, dst, dev):
        k = counter[0]
        counter[0] += 1
        cp = pltpu.make_async_remote_copy(
            src, dst, st_send.at[k], st_recv.at[k], device_id=dev, device_id_type=MESH
        )
        cp.start()
        sends.append(cp)
        return cp

    def rows_for(dx, depth_from, count):
        if dx > 0:
            first = ROWS - (depth_from + count - 1)
            return pl.ds(first, count), pl.ds(DEPTH - (depth_from + count - 1), count)
        return pl.ds(depth_from - 1, count), pl.ds(DEPTH + ROWS + depth_from - 1, count)

    def cols_for(dy):
        if dy > 0:
            return pl.ds(COLS - SIDE, SIDE), pl.ds(0, SIDE)
        if dy < 0:
            return pl.ds(0, SIDE), pl.ds(SIDE + COLS, SIDE)
        return pl.ds(0, COLS), OWN_COLS

    for k in (0, 1, 2, 4, 5):
        loads[k].wait()
    lane8 = lax.broadcasted_iota(jnp.int32, (8, LANES), 1)
    lane1 = lax.broadcasted_iota(jnp.int32, (1, LANES), 1)

    def face_row(i, _):
        vec = jnp.zeros((1, LANES), jnp.int32)
        for jb in range(16):
            seg = ids[i, jb]
            value = tc[seg]
            cols = pl.ds(SIDE + 8 * jb, 8)
            G[DEPTH + i, cols, :] = G[DEPTH + i, cols, :] + jnp.where(lane8 == 0, value, 0.0)
            vec = jnp.where(lane1 == REACH * (jb + 1), seg, vec)
        idrow[i, :, :] = vec
        return 0

    lax.fori_loop(0, ROWS, face_row, 0)

    sub8 = lax.broadcasted_iota(jnp.int32, (8, LANES), 0)
    height = lax.rem(lane8, REACH)
    low, top = height == 0, height == REACH - 1

    def pack_row(i, _):
        b = c = g = b7 = c7 = jnp.zeros((8, LANES), F32)
        for jb in range(16):
            cols = pl.ds(SIDE + 8 * jb, 8)
            at0 = REACH * (jb + 1)
            here = jnp.logical_and(lane8 >= at0, lane8 < at0 + REACH)
            over = lane8 == at0 + REACH
            vb = pltpu.roll(B[DEPTH + i, cols, :], at0, 1)
            vc = pltpu.roll(C[DEPTH + i, cols, :], at0, 1)
            vg = pltpu.roll(G[DEPTH + i, cols, :], at0, 1)
            b, c, g = jnp.where(here, vb, b), jnp.where(here, vc, c), jnp.where(here, vg, g)
            b7, c7 = jnp.where(over, vb, b7), jnp.where(over, vc, c7)
        b7, c7 = pltpu.roll(b7, LANES - 1, 1), pltpu.roll(c7, LANES - 1, 1)
        above = jnp.where(top, c7, pltpu.roll(c, LANES - 1, 1))
        below = jnp.where(low, 0.0, pltpu.roll(c, 1, 1))
        SP[i, 0] = b
        SP[i, 1] = c
        SP[i, 2] = g + c + 0.5 * (above + below)
        SP[i, 3] = jnp.where(top, 0.5 * (c + c7) * b7, 0.0)
        return 0

    lax.fori_loop(0, ROWS, pack_row, 0)
    for side, row0 in ((0, 1), (1, 0)):
        terms = jnp.zeros((8, LANES), F32)
        for k in range(REACH):
            for arr in range(3):
                SB[side, 3 * k + arr] = SP[row0 + k, arr]
            terms = jnp.where(height == k, pltpu.roll(SP[row0 + k, 3], (k - REACH + 1) % LANES, 1), terms)
        SB[side, 3 * REACH] = terms
    HALF = REACH * ROWS
    for side, block in ((0, 16), (1, 1)):
        tiles = [jnp.zeros((8, LANES), F32)] * 2
        for r in range(ROWS):
            for arr, tile, to, width in ((0, 0, REACH * r, REACH), (1, 0, HALF + REACH * r, REACH),
                                         (2, 1, REACH * r, REACH), (3, 1, HALF + r, 1)):
                start = REACH * block + (REACH - 1 if arr == 3 else 0)
                moved = pltpu.roll(SP[r, arr], (to - start) % LANES, 1)
                tiles[tile] = jnp.where(jnp.logical_and(lane8 >= to, lane8 < to + width), moved, tiles[tile])
        ES[side, 0], ES[side, 1] = tiles

    pl.semaphore_wait(barrier, len(partners))

    layer = []
    for dx in (1, -1):
        for side, dy in ((0, 1), (1, -1)):
            layer.append(push(ES.at[side], ER.at[side, dx + 1], at(dx, dy)))
    for side, dx in ((0, 1), (1, -1)):
        layer.append(push(SB.at[side], RB.at[side], at(dx, 0)))
    for side, dy in ((0, 1), (1, -1)):
        layer.append(push(ES.at[side], ER.at[side, 1], at(0, dy)))

    near, first, second = [], [], []
    pairs = ((cot, B), (cond, C))
    first2 = []
    for src, dst in pairs:
        for dy in (1, -1):
            sc, dc = cols_for(dy)
            near.append(push(src.at[:, sc], dst.at[OWN_ROWS, dc], at(0, dy)))
    for dy in (1, -1):
        sc, dc = cols_for(dy)
        src_cols = pl.ds(SIDE + sc.start, sc.size)
        near.append(push(G.at[OWN_ROWS, src_cols], G.at[OWN_ROWS, dc], at(0, dy)))
    for src, dst in pairs:
        for dx in (1, -1):
            for dy in (1, -1):
                sr, dr = rows_for(dx, 1, 3)
                sc, dc = cols_for(dy)
                first.append(push(src.at[sr, sc], dst.at[dr, dc], at(dx, dy)))

    for dx in (1, -1):
        for dy in (1, -1):
            sr, dr = rows_for(dx, 1, 2)
            sc, dc = cols_for(dy)
            first2.append(
                push(
                    G.at[pl.ds(DEPTH + sr.start, 2), pl.ds(SIDE + sc.start, SIDE)],
                    G.at[dr, dc],
                    at(dx, dy),
                )
            )
    for depth, group in ((1, first), (2, first2)):
        for src, dst in pairs:
            for dx in (1, -1):
                sr, dr = rows_for(dx, depth, 1)
                group.append(push(src.at[sr], dst.at[dr, OWN_COLS], at(dx, 0)))
    for dx in (1, -1):
        sr, dr = rows_for(dx, 1, 1)
        first2.append(push(G.at[pl.ds(DEPTH + sr.start, 1), OWN_COLS], G.at[dr, OWN_COLS], at(dx, 0)))
    for src, dst in pairs:
        for dx in (1, -1):
            sr, dr = rows_for(dx, 3, 1)
            second.append(push(src.at[sr], dst.at[dr, OWN_COLS], at(dx, 0)))
    for dx in (1, -1):
        sr, dr = rows_for(dx, 2, 1)
        second.append(push(G.at[pl.ds(DEPTH + sr.start, 1), OWN_COLS], G.at[dr, OWN_COLS], at(dx, 0)))

    inner = (SIDE, SIDE + COLS, SIDE + 8, SIDE + COLS - 8)
    inner2 = (SIDE + 8, SIDE + COLS - 8, SIDE + 16, SIDE + COLS - 16)
    rims = ((0, SIDE + 16, 0, SIDE + 8), (SIDE + COLS - 16, WIDE, SIDE + COLS - 8, WIDE))
    rims2 = ((0, SIDE + 24, 0, SIDE + 16), (SIDE + COLS - 24, WIDE, SIDE + COLS - 16, WIDE))

    def window(span):
        lo, hi, start, stop = span
        return pl.ds(lo, hi - lo), hi - lo, pl.ds(start, stop - start), lambda v: v[start - lo : stop - lo]

    def setup(r, span=(0, WIDE, 0, WIDE)):
        read, width, keep, cut = window(span)
        col = lax.broadcasted_iota(jnp.int32, (span[3] - span[2], LANES), 0) + span[2]
        lane = lax.broadcasted_iota(jnp.int32, (span[3] - span[2], LANES), 1)
        left_edge = jnp.logical_and(col == SIDE, gy == 0)
        right_edge = jnp.logical_and(col == SIDE + COLS - 1, gy == ny - 1)
        line = C[r, read, :]
        centre = cut(line)
        up = jnp.where(jnp.logical_and(r == DEPTH + ROWS - 1, gx == nx - 1), 0.0, C[r + 1, keep, :])
        down = jnp.where(jnp.logical_and(r == DEPTH, gx == 0), 0.0, C[r - 1, keep, :])
        right = jnp.where(right_edge, 0.0, cut(pltpu.roll(line, width - 1, 0)))
        left = jnp.where(left_edge, 0.0, cut(pltpu.roll(line, 1, 0)))
        above = jnp.where(lane == LANES - 1, 0.0, pltpu.roll(centre, LANES - 1, 1))
        below = jnp.where(lane == 0, 0.0, pltpu.roll(centre, 1, 1))
        DG[r, keep, :] = G[r, keep, :] + (
            3.0 * centre + 0.5 * ((up + down) + (right + left) + (above + below))
        )
        WYp[r, keep, :] = jnp.where(right_edge, 0.0, 0.5 * (centre + right))
        WYm[r, keep, :] = jnp.where(left_edge, 0.0, 0.5 * (centre + left))
        WZp[r, keep, :] = jnp.where(lane == LANES - 1, 0.0, 0.5 * (centre + above))
        WZm[r, keep, :] = jnp.where(lane == 0, 0.0, 0.5 * (centre + below))
        outer = jnp.logical_or(
            jnp.logical_and(r == DEPTH + ROWS - 1, gx == nx - 1), jnp.logical_and(r == DEPTH - 1, gx == 0)
        )
        WX[r, keep, :] = jnp.where(outer, 0.0, 0.5 * (centre + up))

    def setup_low(r, keep=pl.ds(0, WIDE)):
        WX[r - 1, keep, :] = jnp.where(
            jnp.logical_and(r == DEPTH, gx == 0), 0.0, 0.5 * (C[r, keep, :] + C[r - 1, keep, :])
        )

    def step(n, r, span):
        a, beta = COEF[n - 1]
        read, width, keep, cut = window(span)
        src = B if n == 1 else X.at[n - 2]
        line = src[r, read, :]
        x = cut(line)
        acc = WX[r, keep, :] * src[r + 1, keep, :] + WX[r - 1, keep, :] * src[r - 1, keep, :]
        acc += WYp[r, keep, :] * cut(pltpu.roll(line, width - 1, 0)) + WYm[r, keep, :] * cut(pltpu.roll(line, 1, 0))
        acc += WZp[r, keep, :] * pltpu.roll(x, LANES - 1, 1) + WZm[r, keep, :] * pltpu.roll(x, 1, 1)
        acc = acc - DG[r, keep, :] * x
        if n == 1:
            return ((1.0 + a) / THETA + beta) * x + (beta / THETA) * acc
        b = B[r, keep, :]
        if n == 2:
            return (1.0 + a) * x + (beta - a / THETA) * b + beta * acc
        return (1.0 + a) * x - a * X[n - 3, r, keep, :] + beta * (b + acc)

    def run(n, rows, span=(0, WIDE, 0, WIDE)):
        for i in rows:
            new = step(n, i + DEPTH, span)
            if n < ITERS - 1:
                X[n - 1, i + DEPTH, pl.ds(span[2], span[3] - span[2]), :] = new
            else:
                out[i] = new[SIDE : SIDE + COLS]

    x_copies = {}

    def send_x(n):
        for side, dx, src_row, dst_row in ((0, 1, 5, 0), (1, -1, 2, TALL - 1)):
            cp = pltpu.make_async_remote_copy(
                X.at[n - 2, DEPTH + src_row], X.at[n - 2, dst_row],
                x_send.at[side, n - 2], x_recv.at[side, n - 2],
                device_id=at(dx, 0), device_id_type=MESH,
            )
            cp.start()
            x_copies[side, n] = cp

    loads[3].wait()
    pick = [jnp.where(lax.rem(lane8, 8) == sub8, gap[i : i + 1, :], 0.0) for i in range(ROWS)]
    target = (lax.broadcasted_iota(jnp.int32, (LANES, LANES), 0) // 8 + 1) * REACH
    place = jnp.where(lax.broadcasted_iota(jnp.int32, (LANES, LANES), 1) == target, 1.0, 0.0).astype(jnp.bfloat16)

    def thirds(value):
        v1 = value.astype(jnp.bfloat16).astype(F32)
        v2 = (value - v1).astype(jnp.bfloat16).astype(F32)
        return jnp.concatenate([v1, v2, value - v1 - v2], axis=0).astype(jnp.bfloat16)

    laid = jnp.dot(thirds(jnp.concatenate(pick, axis=0)), place, preferred_element_type=F32)
    laid = laid[0:64] + laid[64:128] + laid[128:192]
    for i in range(ROWS):
        spread[i] = laid[8 * i : 8 * i + 8, :]

    sub128 = lax.broadcasted_iota(jnp.int32, (LANES, LANES), 0)

    def one_hot(i, _):
        seg = idrow[i]
        low = ((seg >> 5) & 15) * 8 + (seg & 7)
        hot[i] = jnp.where(sub128 == low, 1.0, 0.0).astype(jnp.bfloat16)
        return 0

    lax.fori_loop(0, ROWS, one_hot, 0)

    setup_low(1 + DEPTH, pl.ds(inner[2], inner[3] - inner[2]))
    for i in range(1, 7):
        setup(i + DEPTH, inner)
    run(1, range(1, 7), inner)
    run(2, range(2, 6), inner2)

    for cp in layer:
        cp.wait_recv()
    head = lane8 < REACH
    tail = jnp.logical_and(lane8 >= 17 * REACH, lane8 < 18 * REACH)
    for dx in (-1, 0, 1):
        for r in range(ROWS):
            q = REACH + r - ROWS * dx
            if not 0 <= q < SLAB:
                continue
            for arr, tile, start in ((0, 0, REACH * r), (1, 0, HALF + REACH * r), (2, 1, REACH * r), (3, 1, HALF + r)):
                skip = REACH - 1 if arr == 3 else 0
                if dx == 0:
                    own = SP[r, arr]
                elif arr < 3:
                    own = RB[0 if dx > 0 else 1, 3 * (r - (1 if dx > 0 else 0)) + arr]
                else:
                    k = r - (1 if dx > 0 else 0)
                    own = pltpu.roll(RB[0 if dx > 0 else 1, 3 * REACH], REACH - 1 - k, 1)
                left = pltpu.roll(ER[0, dx + 1, tile], (skip - start) % LANES, 1)
                right = pltpu.roll(ER[1, dx + 1, tile], (17 * REACH + skip - start) % LANES, 1)
                row = jnp.where(head, left, jnp.where(tail, right, own))
                SF[q, arr] = jnp.where(top, row, 0.0) if arr == 3 else row

    def next_col(v):
        t = pltpu.roll(v, 7, 1)
        return jnp.where(lax.broadcasted_iota(jnp.int32, v.shape, 1) == 7, pltpu.roll(t, LANES - REACH, 2), t)

    def last_col(v):
        t = pltpu.roll(v, 1, 1)
        return jnp.where(lax.broadcasted_iota(jnp.int32, v.shape, 1) == 0, pltpu.roll(t, REACH, 2), t)

    def in_block(shape, block):
        spot = lax.broadcasted_iota(jnp.int32, shape, 2)
        return jnp.logical_and(spot >= REACH * block, spot < REACH * (block + 1))

    mid = (SLAB - 2, 8, LANES)
    rows_ = lax.broadcasted_iota(jnp.int32, mid, 0) + 1
    subs_ = lax.broadcasted_iota(jnp.int32, mid, 1)
    high_ = lax.rem(lax.broadcasted_iota(jnp.int32, mid, 2), REACH)
    off_up = jnp.logical_and(rows_ == REACH + ROWS - 1, gx == nx - 1)
    off_down = jnp.logical_and(rows_ == REACH, gx == 0)
    off_right = jnp.logical_and(jnp.logical_and(in_block(mid, 16), subs_ == 7), gy == ny - 1)
    off_left = jnp.logical_and(jnp.logical_and(in_block(mid, 1), subs_ == 0), gy == 0)
    sc_ = SF[1 : SLAB - 1, 1]
    near_cond = [
        jnp.where(off_up, 0.0, SF[2:SLAB, 1]),
        jnp.where(off_down, 0.0, SF[0 : SLAB - 2, 1]),
        jnp.where(off_right, 0.0, next_col(sc_)),
        jnp.where(off_left, 0.0, last_col(sc_)),
    ]
    diag_ = SF[1 : SLAB - 1, 2] + 2.0 * sc_
    weight = []
    for off, other in zip((off_up, off_down, off_right, off_left), near_cond):
        diag_ = diag_ + 0.5 * other
        weight.append(jnp.where(off, 0.0, 0.5 * (sc_ + other)))
    weight.append(jnp.where(high_ == REACH - 1, 0.0, 0.5 * (sc_ + pltpu.roll(sc_, LANES - 1, 2))))
    weight.append(jnp.where(high_ == 0, 0.0, 0.5 * (sc_ + pltpu.roll(sc_, 1, 2))))
    for k, w in enumerate(weight):
        SX[k, 1 : SLAB - 1] = w
    SX[6, 1 : SLAB - 1] = diag_

    for n in range(1, ITERS):
        a, beta = COEF[n - 1]
        lo, hi = n, SLAB - n

        def state(m, p, q):
            return SF[p:q, 0] if m == 1 else SX[5 + m, p:q]

        x = state(n, lo, hi)
        acc = SX[0, lo:hi] * state(n, lo + 1, hi + 1) + SX[1, lo:hi] * state(n, lo - 1, hi - 1)
        acc += SX[2, lo:hi] * next_col(x) + SX[3, lo:hi] * last_col(x)
        acc += SX[4, lo:hi] * pltpu.roll(x, LANES - 1, 2) + SX[5, lo:hi] * pltpu.roll(x, 1, 2)
        acc = acc - SX[6, lo:hi] * x
        b = SF[lo:hi, 0]
        if n == 1:
            new = ((1.0 + a) / THETA + beta) * x + (beta / THETA) * (acc + SF[lo:hi, 3])
        elif n == 2:
            new = (1.0 + a) * x + (beta - a / THETA) * b + beta * acc
        else:
            new = (1.0 + a) * x - a * state(n - 1, lo, hi) + beta * (b + acc)
        if n < ITERS - 1:
            SX[6 + n, lo:hi] = new
    faces = jnp.sum(new * spread[...], axis=1, keepdims=True)

    sub16 = lax.broadcasted_iota(jnp.int32, (16, LANES), 0)
    total = jnp.zeros((48, LANES), F32)
    for i in range(ROWS):
        seg = idrow[i]
        high = (seg >> 9) * 4 + ((seg >> 3) & 3)
        value = jnp.where(sub16 == high, faces[i], 0.0)
        left = thirds(value)
        total = total + lax.dot_general(
            left, hot[i], (((1,), (1,)), ((), ())), preferred_element_type=F32
        )
    sums = total[0:16] + total[16:32] + total[32:48]
    for h in range(16):
        part[h] = sums[h : h + 1, :]

    def all_in(box, sem):
        pltpu.make_async_copy(box.at[pl.ds(1, 15)], box.at[pl.ds(1, 15)], sem).wait()

    for h in plane_order:
        dev = plane(h)
        row = (dev[0] // 16) * 4 + dev[1]
        cp = pltpu.make_async_remote_copy(
            part.at[row], got1.at[h], r_send.at[0], r_recv.at[0], device_id=dev, device_id_type=MESH
        )
        cp.start()
    for cp in near:
        cp.wait_recv()
    for rim in rims:
        setup_low(1 + DEPTH, pl.ds(rim[2], rim[3] - rim[2]))
        for i in range(1, 7):
            setup(i + DEPTH, rim)
        run(1, range(1, 7), rim)
    send_x(2)
    for rim in rims2:
        run(2, range(2, 6), rim)
    send_x(3)
    run(3, (3, 4))

    for cp in first:
        cp.wait_recv()
    setup_low(DEPTH)
    for i in (0, 7):
        setup(i + DEPTH)
    run(1, (0, 7))
    run(2, (1, 6))
    run(3, (2, 5))
    send_x(4)
    for cp in first2:
        cp.wait_recv()
    setup_low(-1 + DEPTH)
    for i in (-1, 8):
        setup(i + DEPTH)
    run(1, (-1, 8))
    run(2, (0, 7))
    run(3, (1, 6))
    run(4, (2, 5))
    send_x(5)
    run(4, (3, 4))
    run(5, (3, 4))

    for cp in second:
        cp.wait_recv()
    setup_low(-2 + DEPTH)
    for i in (-2, 9):
        setup(i + DEPTH)
    run(1, (-2, 9))
    run(2, (-1, 8))
    run(3, (0, 7))
    run(4, (1, 6))
    run(5, (2, 5))
    run(6, (3, 4))

    all_in(got1, r_recv.at[0])
    acc = part[my_y * 4 + gy] + jnp.sum(got1[1:16], axis=0)
    row2[...] = acc
    for h in column_order:
        cp = pltpu.make_async_remote_copy(
            row2, got2.at[h], r_send.at[1], r_recv.at[1], device_id=column(h), device_id_type=MESH
        )
        cp.start()

    for n in (2, 3):
        for side in (0, 1):
            x_copies[side, n].wait_recv()
    run(2, (-2, 9))
    run(3, (-2, -1, 8, 9))
    run(4, (-1, 0, 7, 8))
    run(5, (0, 1, 6, 7))
    run(6, (1, 2, 5, 6))
    run(7, (2, 3, 4, 5))

    for cp in sends:
        cp.wait_send()
    all_in(got1, r_send.at[0])
    for side in (0, 1):
        x_copies[side, 4].wait_recv()
    run(4, (-2, 9))
    run(5, (-1, 8))
    run(6, (0, 7))
    run(7, (1, 6))

    for cp in x_copies.values():
        cp.wait_send()
    for side in (0, 1):
        x_copies[side, 5].wait_recv()
    run(5, (-2, 9))
    run(6, (-1, 8))
    run(7, (0, 7))

    all_in(got2, r_recv.at[1])
    acc = row2[...] + jnp.sum(got2[1:16], axis=0)
    owned = (my_z * 2 + my_c) * 8
    grad[...] = -pltpu.roll(jnp.broadcast_to(acc, (8, LANES)), lax.rem(LANES - owned, LANES), 1)[0, 0:8]

    all_in(got2, r_send.at[1])


def body(cot, cap, cond, gap, tc, ids):
    wide = pltpu.VMEM((TALL, WIDE, LANES), F32)
    n_static = 8 + 4 + 8 + 8 + 2 + 2 + 4 + 4 + 2
    adjoint, grad = pl.pallas_call(
        kernel,
        out_shape=(
            jax.ShapeDtypeStruct((ROWS, COLS, LANES), F32),
            jax.ShapeDtypeStruct((8,), F32),
        ),
        in_specs=[pl.BlockSpec(memory_space=pltpu.HBM)] * 6,
        out_specs=(pl.BlockSpec(memory_space=pltpu.VMEM), pl.BlockSpec(memory_space=pltpu.VMEM)),
        scratch_shapes=[wide] * 9
        + [
            pltpu.VMEM((ITERS - 2, TALL, WIDE, LANES), F32),
            pltpu.VMEM((ROWS, COLS), F32),
            pltpu.SMEM((2048,), F32),
            pltpu.SMEM((ROWS, 16), jnp.int32),
            pltpu.VMEM((ROWS, LANES, LANES), jnp.bfloat16),
            pltpu.VMEM((ROWS, 1, LANES), jnp.int32),
            pltpu.VMEM((ROWS, 8, LANES), F32),
            pltpu.VMEM((16, 1, LANES), F32),
            pltpu.VMEM((16, 1, LANES), F32),
            pltpu.VMEM((1, LANES), F32),
            pltpu.VMEM((16, 1, LANES), F32),
            pltpu.VMEM((ROWS, 4, 8, LANES), F32),
            pltpu.VMEM((SLAB, 4, 8, LANES), F32),
            pltpu.VMEM((2, 3 * REACH + 1, 8, LANES), F32),
            pltpu.VMEM((2, 3 * REACH + 1, 8, LANES), F32),
            pltpu.VMEM((2, 2, 8, LANES), F32),
            pltpu.VMEM((2, 3, 2, 8, LANES), F32),
            pltpu.VMEM((13, SLAB, 8, LANES), F32),
            pltpu.SemaphoreType.DMA((6,)),
            pltpu.SemaphoreType.DMA((n_static,)),
            pltpu.SemaphoreType.DMA((n_static,)),
            pltpu.SemaphoreType.DMA((2, 4)),
            pltpu.SemaphoreType.DMA((2, 4)),
            pltpu.SemaphoreType.DMA((2,)),
            pltpu.SemaphoreType.DMA((2,)),
        ],
        compiler_params=pltpu.CompilerParams(
            collective_id=0, has_side_effects=True, vmem_limit_bytes=48 * 1024 * 1024
        ),
    )(*(pltpu.with_memory_space_constraint(v, pltpu.HBM) for v in (cot, cap, cond, gap, tc, ids)))
    return adjoint, grad


def solution(mesh):
    in_specs = (
        P("gx", "gy", None),
        P("gx", "gy", None),
        P("gx", "gy", None),
        P("gx", "gy"),
        P(),
        P("gx", "gy"),
    )
    out_specs = (P("gx", "gy", None), P(("gx", "gy")))
    return jax.shard_map(body, mesh=mesh, in_specs=in_specs, out_specs=out_specs, check_vma=False)
```
